32 devices in a mesh: patch: 16 (over z, y, core), band: 2 (over x).
Axes of the slice: x: 2, y: 2, z: 4, core: 2. Of those that a mesh axis runs over, the one named last changes fastest.
Arguments:
- tile_flux: bfloat16 [6, 512, 8, 128], P(None, ('patch', 'band')), may hold values from -6 to 6
- tile_weight: bfloat16 [6, 512, 8, 128], P(None, ('patch', 'band')), may hold values from 0.19921875 to 5
- dest_patch: int32 [6, 512], P(None, ('patch', 'band')), may hold values from 0 to 15, as said below
- dest_block: int32 [6, 512], P(None, ('patch', 'band')), may hold values from 0 to 15, as said below
- basis: bfloat16 [2, 21, 31], replicated, may hold values from -1 to 1
- spatial: float32 [16, 6, 3, 21], P('patch'), may hold values from -1.25 to 1.25
Outputs:
- coadd: float32 [16, 64, 512], P('patch', 'band')
The draws below stay inside these ranges and needn't reach their ends.
Inputs may be any that keep to these rules, and one draw needn't show every extreme that they name: `dest_patch`: for each visit, the tiles held by one device go to exactly 8 different patches, 2 tiles to each. `dest_block`: for each visit, every block of every band of every patch receives exactly one tile.
All inputs are finite; a program needn't handle non-finite values.
Results may differ from the reference program's by a relative error of at most 0.0029.
Values may be sent and summed in bfloat16 or wider, within the bound.
No kernel may reach another device: no remote copies, remote signals or barrier semaphores. Data moves between devices by JAX's collectives and lax.ppermute only.
A program may use at most 64 MiB of HBM per device.

```python
import math
import jax
import jax.numpy as jnp
from jax import lax

BASIS = 21
TAPS = 31
VISITS = 6
ROWS = 32
COLS = 512
TILE_ROWS = 8
TILE_COLS = 128
CAP = 2
TILES_V = 16
PATCHES = 16
TILES_ALL = 512
PATCH_ROWS = 64
N_BAND = 2


def shuffled_patches(key):
    count = TILES_V // CAP
    scores = jax.random.permutation(jax.random.fold_in(key, 1), PATCHES).astype(jnp.int32)
    ids = jnp.arange(PATCHES, dtype=jnp.int32)
    scores = jnp.where(ids == 1, -1, scores)
    scores = jnp.where(ids == PATCHES // 2, -2, scores)
    chosen = jnp.argsort(scores, stable=True)[:count].astype(jnp.int32)
    order = jax.random.permutation(jax.random.fold_in(key, 2), count)
    return chosen[order]


def shuffled_blocks(key):
    return jax.random.permutation(key, TILES_V)


def routing_tables(key):
    count = TILES_V // CAP
    shift_keys = jax.random.split(jax.random.fold_in(key, 101), VISITS)
    order_keys = jax.random.split(jax.random.fold_in(key, 202), VISITS)
    shifts = jax.vmap(shuffled_patches)(shift_keys)
    orders = jax.vmap(shuffled_blocks)(order_keys)
    offsets = jax.random.randint(jax.random.fold_in(key, 303), (VISITS, PATCHES), 0, count)
    tile_ids = jnp.arange(TILES_ALL, dtype=jnp.int32)
    source = tile_ids // (N_BAND * TILES_V)
    within = tile_ids % TILES_V
    target = (source[None, :] + shifts[:, within // CAP]) % PATCHES
    lifted = jnp.take_along_axis(offsets, target, axis=1)
    block = jnp.take_along_axis(orders, (within[None, :] + CAP * lifted) % TILES_V, axis=1)
    return (target.astype(jnp.int32), block.astype(jnp.int32))


def draw_dest_patch(key, part):
    return routing_tables(key)[0]


def draw_dest_block(key, part):
    return routing_tables(key)[1]


def shard_levels(stream_key, extent, cuts, low, top_value):
    def one(position, parts):
        draws = jax.random.uniform(jax.random.fold_in(jax.random.fold_in(stream_key, 6), position), (parts,), jnp.float32, low / len(cuts), top_value / len(cuts))
        return jnp.repeat(jnp.exp(draws), extent[position] // parts).reshape((-1,) + (1,) * (len(extent) - position - 1))

    level = one(*cuts[0])
    for cut in cuts[1:]:
        level = level * one(*cut)
    return level


def bell_draw(key, shape, scale, bound, cuts=(), kind=jnp.bfloat16):
    values = scale * jax.random.normal(key, shape, jnp.float32)
    if cuts:
        values = values * shard_levels(key, shape, cuts, -0.22, 0.18)
    return jnp.clip(values, -bound, bound).astype(kind)


def setup_inputs(seed: int = 0) -> dict:
    splits = jax.random.split(jax.random.key(seed), 7)
    return {
        "tile_flux": bell_draw(splits[0], (VISITS, TILES_ALL, TILE_ROWS, TILE_COLS), 1.0, 6.0, ((1, 32),)),
        "tile_weight": jnp.clip(jnp.exp(math.log(5.0) - 3.2227897 * jax.random.uniform(splits[1], (VISITS, TILES_ALL, TILE_ROWS, TILE_COLS), jnp.float32) ** shard_levels(splits[1], (VISITS, TILES_ALL, TILE_ROWS, TILE_COLS), ((1, 32),), -0.2, 0.2)), 0.19921875, 5.0).astype(jnp.bfloat16),
        "dest_patch": draw_dest_patch(jax.random.fold_in(splits[6], 71), 0),
        "dest_block": draw_dest_block(jax.random.fold_in(splits[6], 71), 0),
        "basis": bell_draw(splits[4], (2, BASIS, TAPS), TAPS ** -0.5, 1.0),
        "spatial": bell_draw(splits[5], (PATCHES, VISITS, 3, BASIS), BASIS ** -0.5, 1.25, ((0, 16),), jnp.float32),
    }


def column_table(basis):
    width = 128 + TAPS - 1
    inner = jnp.arange(width)[:, None, None]
    outer = jnp.arange(128)[None, :, None]
    offset = jnp.arange(TAPS)[None, None, :]
    ones = (inner - outer == offset).astype(jnp.float32)
    table = jnp.einsum("iot,bt->ibo", ones, basis[0].astype(jnp.float32))
    return table.reshape(width, BASIS * 128).astype(jnp.bfloat16)


def row_table(basis):
    target = jnp.arange(ROWS)[:, None, None]
    source = jnp.arange(ROWS + TAPS - 1)[None, :, None]
    offset = jnp.arange(TAPS)[None, None, :]
    ones = (source - target == offset).astype(jnp.float32)
    table = jnp.einsum("stk,bk->bst", ones, basis[1].astype(jnp.float32))
    return table.astype(jnp.bfloat16)


def column_filter(rows_block, table):
    margin = TAPS // 2
    padded = jnp.pad(rows_block, ((0, 0), (margin, margin)))
    pieces = jnp.stack([padded[:, 128 * column:128 * column + 128 + TAPS - 1] for column in range(COLS // 128)], axis=1)
    result = jnp.dot(pieces.reshape(-1, 128 + TAPS - 1), table, preferred_element_type=jnp.float32)
    return result.astype(jnp.bfloat16).reshape(rows_block.shape[0], COLS // 128, BASIS, 128)


def reference(tile_flux, tile_weight, dest_patch, dest_block, basis, spatial):
    blocks_across = COLS // TILE_COLS
    margin = TAPS // 2
    tile_ids = jnp.arange(TILES_ALL, dtype=jnp.int32)
    band_of = (tile_ids // TILES_V) % N_BAND
    row_block = dest_block // blocks_across
    col_block = dest_block % blocks_across
    visit_ids = jnp.broadcast_to(jnp.arange(VISITS, dtype=jnp.int32)[:, None], dest_patch.shape)
    band_ids = jnp.broadcast_to(band_of[None, :], dest_patch.shape)
    shape = (VISITS, PATCHES, N_BAND, ROWS // TILE_ROWS, blocks_across, TILE_ROWS, TILE_COLS)
    grid = jnp.zeros(shape, jnp.bfloat16).at[visit_ids, dest_patch, band_ids, row_block, col_block].set(tile_flux)
    frames = grid.transpose(0, 1, 2, 3, 5, 4, 6).reshape(VISITS, PATCHES, PATCH_ROWS, COLS)
    wgrid = jnp.zeros(shape, jnp.float32).at[visit_ids, dest_patch, band_ids, row_block, col_block].set(tile_weight.astype(jnp.float32))
    weight_map = wgrid.transpose(0, 1, 2, 3, 5, 4, 6).reshape(VISITS, PATCHES, PATCH_ROWS, COLS)
    ctable = column_table(basis)
    rtable = row_table(basis).astype(jnp.float32)
    col_coord = ((2.0 * jnp.arange(COLS, dtype=jnp.float32) + 1.0) / COLS - 1.0).reshape(COLS // 128, 128)

    def one_patch(inputs):
        frames_q, weights_q, spatial_q = inputs
        padded = jnp.pad(frames_q, ((0, 0), (margin, margin), (0, 0)))
        filtered = column_filter(padded.reshape(-1, COLS), ctable)
        filtered = filtered.reshape(VISITS, PATCH_ROWS + 2 * margin, COLS // 128, BASIS, 128)
        pieces = []
        for band in range(N_BAND):
            part = filtered[:, band * ROWS:band * ROWS + ROWS + 2 * margin].astype(jnp.float32)
            smoothed = jnp.einsum("bst,vtcbo->vscbo", rtable, part)
            mixture = jnp.einsum("vscbo,vjb->vjsco", smoothed, spatial_q, precision=lax.Precision.HIGHEST)
            row_coord = (2.0 * (band * ROWS + jnp.arange(ROWS, dtype=jnp.float32)) + 1.0) / PATCH_ROWS - 1.0
            matched = mixture[:, 0] + row_coord[None, :, None, None] * mixture[:, 1] + col_coord[None, None] * mixture[:, 2]
            pieces.append(matched.reshape(VISITS, ROWS, COLS))
        matched = jnp.concatenate(pieces, axis=1)
        return jnp.sum(weights_q * matched, axis=0) / jnp.sum(weights_q, axis=0)

    return lax.map(one_patch, (frames.transpose(1, 0, 2, 3), weight_map.transpose(1, 0, 2, 3), spatial))
```

```python
import jax
import jax.numpy as jnp
from jax import lax
from jax.experimental import pallas as pl
from jax.experimental.pallas import tpu as pltpu
from jax.sharding import PartitionSpec as P

BASIS = 21
GROUPS = 24
TAPS = 31
MARGIN = TAPS // 2
ROWS = 32
COLS = 512
TILE_ROWS = 8
LANES = 128
ACROSS = COLS // LANES
DOWN = ROWS // TILE_ROWS
CAP = 2
HALO = 16
PAIR = 2 * LANES
F32 = jnp.float32
BF16 = jnp.bfloat16
I32 = jnp.int32


def iota(shape, dim):
    return lax.broadcasted_iota(I32, shape, dim)


def vmem():
    return pl.BlockSpec(memory_space=pltpu.VMEM)


def smem():
    return pl.BlockSpec(memory_space=pltpu.SMEM)


def params():
    return pltpu.CompilerParams(vmem_limit_bytes=40 * 1024 * 1024)


def cost(flops, moved):
    return pl.CostEstimate(flops=flops, bytes_accessed=moved, transcendentals=0)


def slots_of(dest):
    count = dest.shape[1]
    lane = iota(dest.shape, 1)
    ordinal = jnp.zeros(dest.shape, I32)
    for t in range(count - 1):
        same = jnp.logical_and(dest == dest[:, t : t + 1], lane > t)
        ordinal = ordinal + jnp.where(same, 1, 0)
    return dest * CAP + ordinal, ordinal


def spread(values, width, repeat):
    m = values.shape[1]
    hot = (iota((m, width), 1) // repeat == iota((m, width), 0)).astype(F32).astype(BF16)
    return jnp.dot(values.astype(F32).astype(BF16), hot, preferred_element_type=F32).astype(I32)


def pack(dest, tiles_ref, out_ref):
    visits, depth, _ = tiles_ref.shape
    patches = out_ref.shape[0]
    block = CAP * TILE_ROWS
    slot, _ = slots_of(dest)
    goal = spread(slot, depth, TILE_ROWS) * TILE_ROWS + iota((visits, depth), 1) % TILE_ROWS
    row = iota((patches * block, depth), 0)
    for k in range(visits):
        hot = jnp.where(row == goal[k : k + 1], 1.0, 0.0).astype(BF16)
        moved = jnp.dot(hot, tiles_ref[k], preferred_element_type=F32).astype(BF16)
        out_ref[:, k * block : (k + 1) * block, :] = moved.reshape(patches, block, LANES)


def pack_flux_kernel(me_ref, dest_ref, block_ref, tiles_ref, out_ref):
    dest = dest_ref[...]
    visits = dest.shape[0]
    patches = out_ref.shape[0]
    pack(dest, tiles_ref, out_ref)
    _, ordinal = slots_of(dest)
    place = block_ref[...] % ACROSS * DOWN + block_ref[...] // ACROSS + 1
    lane = iota((TILE_ROWS, LANES), 1)
    first = CAP * me_ref[0]
    for q in range(patches):
        note = jnp.zeros((TILE_ROWS, LANES), F32)
        for o in range(CAP):
            chosen = jnp.logical_and(dest == q, ordinal == o)
            value = jnp.sum(jnp.where(chosen, place, 0).astype(F32), axis=1, keepdims=True)
            value = jnp.concatenate([value, jnp.zeros((TILE_ROWS - visits, 1), F32)], axis=0)
            note = jnp.where(lane == first + o, value, note)
        out_ref[q, visits * CAP * TILE_ROWS :, :] = note.astype(BF16)


def pack_weight_kernel(dest_ref, tiles_ref, out_ref):
    pack(dest_ref[...], tiles_ref, out_ref)


def placing(note, senders):
    width = senders * CAP * TILE_ROWS
    hot = (iota((LANES, width), 1) // TILE_ROWS == iota((LANES, width), 0)).astype(F32).astype(BF16)
    place = jnp.dot(note.astype(BF16), hot, preferred_element_type=F32).astype(I32) - 1
    return place * TILE_ROWS + iota((TILE_ROWS, width), 1) % TILE_ROWS


def placed(goal, received):
    hot = jnp.where(iota((ACROSS * ROWS, goal.shape[1]), 0) == goal, 1.0, 0.0).astype(BF16)
    return jnp.dot(hot, received, preferred_element_type=F32)


def place_kernel(recv_ref, frame_ref, top_ref, bottom_ref, note_ref):
    senders = recv_ref.shape[0]
    visits = frame_ref.shape[0]
    block = CAP * TILE_ROWS
    note = jnp.sum(recv_ref[:, visits * block :, :].astype(F32), axis=0)
    note_ref[...] = note
    goal = placing(note, senders)
    for k in range(visits):
        received = recv_ref[:, k * block : (k + 1) * block, :].reshape(senders * block, LANES)
        frame = placed(goal[k : k + 1], received).astype(BF16).reshape(ACROSS, ROWS, LANES)
        frame_ref[k] = frame
        top_ref[k] = frame[:, :HALO]
        bottom_ref[k] = frame[:, ROWS - HALO :]


def hot_rows(taps, shift_lane, width, used=None):
    lane = iota((TAPS, width), 1)
    tap = iota((TAPS, width), 0)
    hot = lane == shift_lane(tap)
    if used is not None:
        hot = jnp.logical_and(hot, used(tap))
    hot = hot.astype(F32).astype(BF16)
    return jnp.dot(taps, hot, preferred_element_type=F32)


def table_kernel(first_ref, up_ref, column_ref, row_ref, spatial_ref, coord_ref, table_ref, own_ref, halo_ref):
    low = LANES // 2 - MARGIN
    lines = hot_rows(column_ref[...], lambda tap: (-low - tap) % LANES, LANES)
    gap = iota((PAIR, LANES), 0) - iota((PAIR, LANES), 1) - low
    inside = jnp.logical_and(gap >= 0, gap < TAPS)
    for b in range(table_ref.shape[1] // LANES):
        if b < BASIS:
            line = jnp.broadcast_to(lines[b : b + 1], (PAIR, LANES))
            rolled = pltpu.roll(line, 0, 1, stride=1, stride_axis=0)
            part = jnp.where(inside, rolled, 0.0)
        else:
            part = jnp.zeros((PAIR, LANES), F32)
        table_ref[:, b * LANES : (b + 1) * LANES] = part.astype(BF16)

    visits = own_ref.shape[0]
    coord = coord_ref[...]
    spatial = spatial_ref[...]

    def fill(out_ref, height, offset, used=None):
        fit = LANES // height
        line = 0.0
        which = iota((GROUPS, LANES), 0)
        for j in range(fit):
            part = hot_rows(
                row_ref[...], lambda tap: (height * j + tap - offset + 2 * LANES) % LANES, LANES, used
            )
            line = line + jnp.where(which % fit == j, part, 0.0)
        t = iota((ROWS, LANES), 1) % height
        tap = t - iota((ROWS, LANES), 0) + offset
        good = jnp.logical_and(tap >= 0, tap < TAPS)
        width = GROUPS * height
        hot = (iota((BASIS, width), 1) // height == iota((BASIS, width), 0)).astype(F32)
        coef = jnp.dot(spatial, hot, precision=lax.Precision.HIGHEST, preferred_element_type=F32)
        for g in range(GROUPS // fit):
            here = jnp.sum(line[g * fit : (g + 1) * fit], axis=0, keepdims=True)
            rolled = pltpu.roll(jnp.broadcast_to(here, (ROWS, LANES)), 0, 1, stride=1, stride_axis=0)
            taps = jnp.where(good, rolled, 0.0)
            lanes = slice(g * LANES, (g + 1) * LANES)
            for k in range(visits):
                c = coef[3 * k : 3 * k + 3, lanes]
                out_ref[k, :ROWS, lanes] = ((c[0:1] + coord * c[1:2]) * taps).astype(BF16)
                out_ref[k, ROWS:, lanes] = (c[2:3] * taps).astype(BF16)

    fill(own_ref, ROWS, MARGIN)
    up = up_ref[0] > 0
    low = jnp.where(up, 0, MARGIN + 1)
    fill(
        halo_ref,
        HALO,
        jnp.where(up, MARGIN - HALO, MARGIN + ROWS),
        lambda tap: jnp.logical_and(tap >= low, tap < low + MARGIN),
    )


def filter_kernel(frame_ref, table_ref, mix_ref, out_ref, windows, filtered):
    visits, _, height, _ = frame_ref.shape
    half = LANES // 2
    left = iota((height, LANES), 1) < half
    count = ACROSS * height
    for k in range(visits):
        rolled = [pltpu.roll(frame_ref[k, c].astype(F32), half, 1) for c in range(ACROSS)]
        zero = jnp.zeros((height, LANES), F32)
        padded = [zero] + rolled + [zero]
        pieces = [jnp.where(left, padded[c], padded[c + 1]).astype(BF16) for c in range(ACROSS + 1)]
        for c in range(ACROSS):
            rows = slice(k * count + c * height, k * count + (c + 1) * height)
            windows[rows, :LANES] = pieces[c]
            windows[rows, LANES:] = pieces[c + 1]
    done = table_ref.shape[1] // LANES
    filtered[:, done * height :, :] = jnp.zeros((visits, filtered.shape[1] - done * height, COLS), BF16)
    for p in range(done // 2):
        part = jnp.dot(windows[...], table_ref[:, p * PAIR : (p + 1) * PAIR], preferred_element_type=F32).astype(BF16)
        for k in range(visits):
            for c in range(ACROSS):
                for j in range(2):
                    b = 2 * p + j
                    filtered[k, b * height : (b + 1) * height, c * LANES : (c + 1) * LANES] = part[
                        k * count + c * height : k * count + (c + 1) * height, j * LANES : (j + 1) * LANES
                    ]
    col = (2.0 * iota((1, COLS), 1).astype(F32) + 1.0) / COLS - 1.0
    for k in range(visits):
        both = jnp.dot(mix_ref[k], filtered[k], preferred_element_type=F32)
        out_ref[k] = both[:ROWS] + col * both[ROWS:]


def final_kernel(note_ref, recv_ref, *refs):
    parts, out_ref = refs[:-1], refs[-1]
    senders = recv_ref.shape[0]
    visits = parts[0].shape[0]
    block = CAP * TILE_ROWS
    goal = placing(note_ref[...], senders)
    total = jnp.zeros((ACROSS * ROWS, LANES), F32)
    sums = [jnp.zeros((ROWS, LANES), F32) for _ in range(ACROSS)]
    for k in range(visits):
        received = recv_ref[:, k * block : (k + 1) * block, :].reshape(senders * block, LANES)
        weight = placed(goal[k : k + 1], received)
        total = total + weight
        for c in range(ACROSS):
            lanes = slice(c * LANES, (c + 1) * LANES)
            value = parts[0][k, :, lanes]
            for other in parts[1:]:
                value = value + other[k, :, lanes]
            sums[c] = sums[c] + weight[c * ROWS : (c + 1) * ROWS] * value
    for c in range(ACROSS):
        out_ref[0, :, c * LANES : (c + 1) * LANES] = sums[c] / total[c * ROWS : (c + 1) * ROWS]


def shape(dims, kind):
    return jax.ShapeDtypeStruct(dims, kind)


def filter_rows(frame, table, mix, name):
    visits, _, height, _ = frame.shape
    return pl.pallas_call(
        filter_kernel,
        out_shape=shape((visits, ROWS, COLS), F32),
        in_specs=[vmem()] * 3,
        out_specs=vmem(),
        scratch_shapes=[
            pltpu.VMEM((visits * ACROSS * height, PAIR), BF16),
            pltpu.VMEM((visits, GROUPS * height, COLS), BF16),
        ],
        compiler_params=params(),
        cost_estimate=cost(4 * visits * ACROSS * height * PAIR * BASIS * LANES, 4 * 1024 * 1024),
        name=name,
    )(frame, table, mix)


def per_device(tile_flux, tile_weight, dest_patch, dest_block, basis, spatial):
    visits, tile_count, tile_height, tile_width = tile_flux.shape
    patches, bands = lax.axis_size("patch"), lax.axis_size("band")
    me, band = lax.axis_index("patch"), lax.axis_index("band")
    depth = tile_count * tile_height
    block = CAP * TILE_ROWS
    flux = tile_flux.reshape(visits, depth, tile_width)
    weight = tile_weight.reshape(visits, depth, tile_width)
    send_flux = pl.pallas_call(
        pack_flux_kernel,
        out_shape=shape((patches, visits * block + TILE_ROWS, LANES), BF16),
        in_specs=[smem()] + [vmem()] * 3,
        out_specs=vmem(),
        compiler_params=params(),
        name="pack_flux",
    )(me.reshape(1), dest_patch, dest_block, flux)
    send_weight = pl.pallas_call(
        pack_weight_kernel,
        out_shape=shape((patches, visits * block, LANES), BF16),
        in_specs=[vmem()] * 2,
        out_specs=vmem(),
        compiler_params=params(),
        name="pack_weight",
    )(dest_patch, weight)
    recv_flux = lax.all_to_all(send_flux, "patch", split_axis=0, concat_axis=0, tiled=True)
    recv_weight = lax.all_to_all(send_weight, "patch", split_axis=0, concat_axis=0, tiled=True)

    row = (band * ROWS).astype(F32) + jnp.arange(ROWS, dtype=F32)
    coord = jnp.broadcast_to(((2.0 * row + 1.0) / (ROWS * bands) - 1.0)[:, None], (ROWS, LANES))
    taps = jnp.pad(basis, ((0, 0), (0, GROUPS - BASIS), (0, 0)))
    coefs = spatial[0].reshape(visits * 3, BASIS)

    def tables(up):
        return pl.pallas_call(
            table_kernel,
            out_shape=(
                shape((PAIR, 2 * pl.cdiv(BASIS, 2) * LANES), BF16),
                shape((visits, 2 * ROWS, GROUPS * ROWS), BF16),
                shape((visits, 2 * ROWS, GROUPS * HALO), BF16),
            ),
            in_specs=[smem()] * 2 + [vmem()] * 4,
            out_specs=(vmem(),) * 3,
            compiler_params=params(),
            cost_estimate=cost(10**9, 4 * 1024 * 1024),
            name="tables",
        )(band.reshape(1), up.reshape(1).astype(I32), taps[0], taps[1], coefs, coord)

    frame, top, bottom, note = pl.pallas_call(
        place_kernel,
        out_shape=(
            shape((visits, ACROSS, ROWS, LANES), BF16),
            shape((visits, ACROSS, HALO, LANES), BF16),
            shape((visits, ACROSS, HALO, LANES), BF16),
            shape((TILE_ROWS, LANES), F32),
        ),
        in_specs=[vmem()],
        out_specs=(vmem(),) * 4,
        compiler_params=params(),
        name="place_flux",
    )(recv_flux)

    if bands == 2:
        edge = jnp.where(band == 0, bottom, top)
        halos = [lax.ppermute(edge, "band", [(0, 1), (1, 0)])]
        ups = [band]
    else:
        down = [(i, i + 1) for i in range(bands - 1)]
        halos = [
            lax.ppermute(bottom, "band", down),
            lax.ppermute(top, "band", [(j, i) for i, j in down]),
        ]
        ups = [jnp.int32(1), jnp.int32(0)]
    built = [tables(up) for up in ups]
    table, own_mix, _ = built[0]
    parts = [filter_rows(frame, table, own_mix, "filter_own")]
    for halo, (_, _, halo_mix) in zip(halos, built):
        parts.append(filter_rows(halo, table, halo_mix, "filter_halo"))
    return pl.pallas_call(
        final_kernel,
        out_shape=shape((1, ROWS, COLS), F32),
        in_specs=[vmem()] * (2 + len(parts)),
        out_specs=vmem(),
        compiler_params=params(),
        name="final",
    )(note, recv_weight, *parts)


def solution(mesh):
    in_specs = (
        P(None, ("patch", "band"), None, None),
        P(None, ("patch", "band"), None, None),
        P(None, ("patch", "band")),
        P(None, ("patch", "band")),
        P(),
        P("patch", None, None, None),
    )
    out_specs = P("patch", "band", None)
    return jax.shard_map(
        per_device, mesh=mesh, in_specs=in_specs, out_specs=out_specs, check_vma=False
    )
```

```python
import functools

import jax
import jax.numpy as jnp
from jax import lax
from jax.experimental import pallas as pl
from jax.experimental.pallas import tpu as pltpu
from jax.sharding import PartitionSpec as P

BASIS = 21
GROUPS = 24
TAPS = 31
MARGIN = TAPS // 2
ROWS = 32
COLS = 512
TILE_ROWS = 8
LANES = 128
ACROSS = COLS // LANES
DOWN = ROWS // TILE_ROWS
CAP = 2
NEAR = 4
HALO = 16
PAIR = 2 * LANES
F32 = jnp.float32
BF16 = jnp.bfloat16
I32 = jnp.int32


def iota(shape, dim):
    return lax.broadcasted_iota(I32, shape, dim)


def vmem():
    return pl.BlockSpec(memory_space=pltpu.VMEM)


def smem():
    return pl.BlockSpec(memory_space=pltpu.SMEM)


def params(mib=40):
    return pltpu.CompilerParams(vmem_limit_bytes=mib * 1024 * 1024)


def cost(flops, moved):
    return pl.CostEstimate(flops=flops, bytes_accessed=moved, transcendentals=0)


def slots_of(dest):
    count = dest.shape[1]
    lane = iota(dest.shape, 1)
    ordinal = jnp.zeros(dest.shape, I32)
    for t in range(count - 1):
        same = jnp.logical_and(dest == dest[:, t : t + 1], lane > t)
        ordinal = ordinal + jnp.where(same, 1, 0)
    return dest * CAP + ordinal


def spread(values, width, repeat):
    m = values.shape[1]
    hot = (iota((m, width), 1) // repeat == iota((m, width), 0)).astype(F32).astype(BF16)
    return jnp.dot(values.astype(F32).astype(BF16), hot, preferred_element_type=F32).astype(I32)


def start_copies(pairs, sems):
    copies = [pltpu.make_async_copy(src, dst, sems.at[i]) for i, (src, dst) in enumerate(pairs)]
    for copy in copies:
        copy.start()
    return copies


def sort_visit(goal, tiles, slots):
    row = iota((slots * TILE_ROWS, goal.shape[1]), 0)
    hot = jnp.where(row == goal, 1.0, 0.0).astype(BF16)
    return jnp.dot(hot, tiles, preferred_element_type=F32).astype(BF16)


def pack_kernel(far, dest_hbm, block_hbm, flux_hbm, weight_hbm, *refs):
    flux_out, weight_out = refs[:far], refs[far : far + NEAR]
    landing, sems = refs[far + NEAR : -1], refs[-1]
    copies = start_copies(zip((dest_hbm, block_hbm, flux_hbm, weight_hbm), landing), sems)
    dest_ref, block_ref, flux_ref, weight_ref = landing
    visits, depth, _ = flux_ref.shape
    block = CAP * TILE_ROWS
    copies[0].wait()
    copies[1].wait()
    slot = slots_of(jnp.bitwise_xor(dest_ref[...], lax.axis_index("patch")))
    goal = spread(slot, depth, TILE_ROWS) * TILE_ROWS + iota((visits, depth), 1) % TILE_ROWS
    place = block_ref[...] % ACROSS * DOWN + block_ref[...] // ACROSS + 1
    lane = iota((TILE_ROWS, LANES), 1)
    for x in range(far):
        for y in range(NEAR):
            note = jnp.zeros((TILE_ROWS, LANES), F32)
            for o in range(CAP):
                chosen = slot == CAP * (x * NEAR + y) + o
                value = jnp.sum(jnp.where(chosen, place, 0).astype(F32), axis=1, keepdims=True)
                value = jnp.concatenate([value, jnp.zeros((TILE_ROWS - visits, 1), F32)], axis=0)
                note = jnp.where(lane == CAP * (y * far + x) + o, value, note)
            flux_out[x][y, visits * block :, :] = note.astype(BF16)
    copies[2].wait()
    copies[3].wait()
    for k in range(visits):
        both = jnp.concatenate([flux_ref[k], weight_ref[k]], axis=1)
        moved = sort_visit(goal[k : k + 1], both, far * NEAR * CAP)
        lines = slice(k * block, (k + 1) * block)
        for x in range(far):
            for y in range(NEAR):
                rel = x * NEAR + y
                part = moved[rel * block : (rel + 1) * block]
                flux_out[x][y, lines, :] = part[:, :LANES]
                weight_out[y][x, lines, :] = part[:, LANES:]


def regroup_kernel(count, backward, *refs):
    ins = refs[:count][:: -1 if backward else 1]
    outs = refs[-(ins[0].shape[0] - 1) :]
    for j, out in enumerate(outs):
        for i, part in enumerate(ins):
            out[i] = part[j + 1]


def placing(note, senders):
    width = senders * CAP * TILE_ROWS
    hot = (iota((LANES, width), 1) // TILE_ROWS == iota((LANES, width), 0)).astype(F32).astype(BF16)
    place = jnp.dot(note.astype(BF16), hot, preferred_element_type=F32).astype(I32) - 1
    return place * TILE_ROWS + iota((TILE_ROWS, width), 1) % TILE_ROWS


def placed(goal, received):
    hot = jnp.where(iota((ACROSS * ROWS, goal.shape[1]), 0) == goal, 1.0, 0.0).astype(BF16)
    return jnp.dot(hot, received, preferred_element_type=F32)


def place_kernel(far, swap, *refs):
    chunks, others = refs[:far][::-1], refs[far : far + NEAR - 1]
    frame_ref, note_ref, *edges = refs[far + NEAR - 1 :]
    visits = frame_ref.shape[0]
    block = CAP * TILE_ROWS
    note = sum(chunk[0, visits * block :, :].astype(F32) for chunk in chunks)
    for other in others:
        note = note + jnp.sum(other[:, visits * block :, :].astype(F32), axis=0)
    note_ref[...] = note
    goal = placing(note, far * NEAR)
    for k in range(visits):
        lines = slice(k * block, (k + 1) * block)
        received = [chunk[0, lines, :] for chunk in chunks]
        received += [other[:, lines, :].reshape(far * block, LANES) for other in others]
        frame = placed(goal[k : k + 1], jnp.concatenate(received, axis=0)).astype(BF16)
        frame = frame.reshape(ACROSS, ROWS, LANES)
        frame_ref[k] = frame
        top, bottom = frame[:, :HALO], frame[:, ROWS - HALO :]
        if swap:
            edges[0][k] = jnp.where(lax.axis_index("band") == 0, bottom, top)
        else:
            edges[0][k] = top
            edges[1][k] = bottom


def hot_rows(taps, shift_lane, width, used=None):
    lane = iota((TAPS, width), 1)
    tap = iota((TAPS, width), 0)
    hot = lane == shift_lane(tap)
    if used is not None:
        hot = jnp.logical_and(hot, used(tap))
    hot = hot.astype(F32).astype(BF16)
    return jnp.dot(taps, hot, preferred_element_type=F32)


def table_kernel(bands, up_ref, taps_ref, spatial_ref, table_ref, own_ref, halo_ref):
    taps = [taps_ref[b].astype(F32) for b in range(BASIS)]
    blank = [jnp.zeros((GROUPS - BASIS, TAPS), F32)]
    column, line_taps = (
        jnp.concatenate([tap[i : i + 1] for tap in taps] + blank, axis=0).astype(BF16) for i in range(2)
    )
    low = LANES // 2 - MARGIN
    lines = hot_rows(column, lambda tap: (-low - tap) % LANES, LANES)
    gap = iota((PAIR, LANES), 0) - iota((PAIR, LANES), 1) - low
    inside = jnp.logical_and(gap >= 0, gap < TAPS)
    for b in range(table_ref.shape[1] // LANES):
        if b < BASIS:
            line = jnp.broadcast_to(lines[b : b + 1], (PAIR, LANES))
            rolled = pltpu.roll(line, 0, 1, stride=1, stride_axis=0)
            part = jnp.where(inside, rolled, 0.0)
        else:
            part = jnp.zeros((PAIR, LANES), F32)
        table_ref[:, b * LANES : (b + 1) * LANES] = part.astype(BF16)

    visits = own_ref.shape[0]
    row = lax.axis_index("band") * ROWS + iota((ROWS, LANES), 0)
    coord = (2.0 * row.astype(F32) + 1.0) / (ROWS * bands) - 1.0
    spatial = jnp.concatenate([spatial_ref[i] for i in range(3 * visits)], axis=0)

    def fill(out_ref, height, offset, used=None):
        fit = LANES // height
        line = 0.0
        which = iota((GROUPS, LANES), 0)
        for j in range(fit):
            part = hot_rows(
                line_taps, lambda tap: (height * j + tap - offset + 2 * LANES) % LANES, LANES, used
            )
            line = line + jnp.where(which % fit == j, part, 0.0)
        t = iota((ROWS, LANES), 1) % height
        tap = t - iota((ROWS, LANES), 0) + offset
        good = jnp.logical_and(tap >= 0, tap < TAPS)
        width = GROUPS * height
        hot = (iota((BASIS, width), 1) // height == iota((BASIS, width), 0)).astype(F32)
        coef = jnp.dot(spatial, hot, precision=lax.Precision.HIGHEST, preferred_element_type=F32)
        for g in range(GROUPS // fit):
            here = jnp.sum(line[g * fit : (g + 1) * fit], axis=0, keepdims=True)
            rolled = pltpu.roll(jnp.broadcast_to(here, (ROWS, LANES)), 0, 1, stride=1, stride_axis=0)
            taps = jnp.where(good, rolled, 0.0)
            lanes = slice(g * LANES, (g + 1) * LANES)
            for k in range(visits):
                c = coef[3 * k : 3 * k + 3, lanes]
                out_ref[k, :ROWS, lanes] = ((c[0:1] + coord * c[1:2]) * taps).astype(BF16)
                out_ref[k, ROWS:, lanes] = (c[2:3] * taps).astype(BF16)

    fill(own_ref, ROWS, MARGIN)
    up = up_ref[0] > 0
    low = jnp.where(up, 0, MARGIN + 1)
    fill(
        halo_ref,
        HALO,
        jnp.where(up, MARGIN - HALO, MARGIN + ROWS),
        lambda tap: jnp.logical_and(tap >= low, tap < low + MARGIN),
    )


def filter_kernel(frame_ref, table_ref, mix_ref, out_ref, windows, filtered):
    visits, _, height, _ = frame_ref.shape
    half = LANES // 2
    left = iota((height, LANES), 1) < half
    count = ACROSS * height
    for k in range(visits):
        rolled = [pltpu.roll(frame_ref[k, c].astype(F32), half, 1) for c in range(ACROSS)]
        zero = jnp.zeros((height, LANES), F32)
        padded = [zero] + rolled + [zero]
        pieces = [jnp.where(left, padded[c], padded[c + 1]).astype(BF16) for c in range(ACROSS + 1)]
        for c in range(ACROSS):
            rows = slice(k * count + c * height, k * count + (c + 1) * height)
            windows[rows, :LANES] = pieces[c]
            windows[rows, LANES:] = pieces[c + 1]
    done = table_ref.shape[1] // LANES
    filtered[:, done * height :, :] = jnp.zeros((visits, filtered.shape[1] - done * height, COLS), BF16)
    for p in range(done // 2):
        part = jnp.dot(windows[...], table_ref[:, p * PAIR : (p + 1) * PAIR], preferred_element_type=F32).astype(BF16)
        for k in range(visits):
            for c in range(ACROSS):
                for j in range(2):
                    b = 2 * p + j
                    filtered[k, b * height : (b + 1) * height, c * LANES : (c + 1) * LANES] = part[
                        k * count + c * height : k * count + (c + 1) * height, j * LANES : (j + 1) * LANES
                    ]
    col = (2.0 * iota((1, COLS), 1).astype(F32) + 1.0) / COLS - 1.0
    for k in range(visits):
        both = jnp.dot(mix_ref[k], filtered[k], preferred_element_type=F32)
        out_ref[k] = both[:ROWS] + col * both[ROWS:]


def final_kernel(far, note_ref, *refs):
    chunks, others = refs[:NEAR], refs[NEAR : NEAR + far - 1][::-1]
    parts, out_ref = refs[NEAR + far - 1 : -1], refs[-1]
    visits = parts[0].shape[0]
    block = CAP * TILE_ROWS
    goal = placing(note_ref[...], far * NEAR)
    total = jnp.zeros((ACROSS * ROWS, LANES), F32)
    sums = [jnp.zeros((ROWS, LANES), F32) for _ in range(ACROSS)]
    for k in range(visits):
        lines = slice(k * block, (k + 1) * block)
        received = []
        for y in range(NEAR):
            received += [chunks[y][0, lines, :]] + [other[y, lines, :] for other in others]
        weight = placed(goal[k : k + 1], jnp.concatenate(received, axis=0))
        total = total + weight
        for c in range(ACROSS):
            lanes = slice(c * LANES, (c + 1) * LANES)
            value = parts[0][k, :, lanes]
            for other in parts[1:]:
                value = value + other[k, :, lanes]
            sums[c] = sums[c] + weight[c * ROWS : (c + 1) * ROWS] * value
    for c in range(ACROSS):
        out_ref[0, :, c * LANES : (c + 1) * LANES] = sums[c] / total[c * ROWS : (c + 1) * ROWS]


def shape(dims, kind):
    return jax.ShapeDtypeStruct(dims, kind)


def filter_rows(frame, table, mix, name):
    visits, _, height, _ = frame.shape
    return pl.pallas_call(
        filter_kernel,
        out_shape=shape((visits, ROWS, COLS), F32),
        in_specs=[vmem()] * 3,
        out_specs=vmem(),
        scratch_shapes=[
            pltpu.VMEM((visits * ACROSS * height, PAIR), BF16),
            pltpu.VMEM((visits, GROUPS * height, COLS), BF16),
        ],
        compiler_params=params(),
        cost_estimate=cost(4 * visits * ACROSS * height * PAIR * BASIS * LANES, 4 * 1024 * 1024),
        name=name,
    )(frame, table, mix)


def regroup(parts, after, name, backward=False):
    count = parts[0].shape[0]
    return pl.pallas_call(
        functools.partial(regroup_kernel, len(parts), backward),
        out_shape=tuple(shape((len(parts),) + parts[0].shape[1:], BF16) for _ in range(count - 1)),
        in_specs=[vmem()] * len(parts) + [pl.BlockSpec(memory_space=pl.ANY)] * len(after),
        out_specs=(vmem(),) * (count - 1),
        compiler_params=params(),
        name=name,
    )(*parts, *after)


def per_device(tile_flux, tile_weight, dest_patch, dest_block, basis, spatial):
    visits, tile_count, tile_height, tile_width = tile_flux.shape
    patches, bands = lax.axis_size("patch"), lax.axis_size("band")
    band = lax.axis_index("band")
    far = patches // NEAR
    depth = tile_count * tile_height
    block = CAP * TILE_ROWS
    flux = tile_flux.reshape(visits, depth, tile_width)
    weight = tile_weight.reshape(visits, depth, tile_width)

    def swap(value, step):
        return lax.ppermute(value, "patch", [(i, i ^ step) for i in range(patches)])

    packed = pl.pallas_call(
        functools.partial(pack_kernel, far),
        out_shape=(shape((NEAR, visits * block + TILE_ROWS, LANES), BF16),) * far
        + (shape((far, visits * block, LANES), BF16),) * NEAR,
        in_specs=[pl.BlockSpec(memory_space=pltpu.HBM)] * 4,
        out_specs=(vmem(),) * (far + NEAR),
        scratch_shapes=[
            pltpu.VMEM(dest_patch.shape, I32),
            pltpu.VMEM(dest_block.shape, I32),
            pltpu.VMEM(flux.shape, BF16),
            pltpu.VMEM(weight.shape, BF16),
            pltpu.SemaphoreType.DMA((4,)),
        ],
        compiler_params=params(60),
        name="pack",
    )(dest_patch, dest_block, flux, weight)
    flux_far = [swap(packed[x], x * NEAR) for x in range(far - 1, 0, -1)] + [packed[0]]
    weight_near = [packed[far]] + [swap(packed[far + y], y) for y in range(1, NEAR)]

    coefs = spatial.reshape(visits * 3, 1, BASIS)
    taps = basis.transpose(1, 0, 2)

    def tables(up):
        return pl.pallas_call(
            functools.partial(table_kernel, bands),
            out_shape=(
                shape((PAIR, 2 * pl.cdiv(BASIS, 2) * LANES), BF16),
                shape((visits, 2 * ROWS, GROUPS * ROWS), BF16),
                shape((visits, 2 * ROWS, GROUPS * HALO), BF16),
            ),
            in_specs=[smem()] + [vmem()] * 2,
            out_specs=(vmem(),) * 3,
            compiler_params=params(),
            cost_estimate=cost(10**9, 4 * 1024 * 1024),
            name="tables",
        )(up.reshape(1).astype(I32), taps, coefs)

    if bands == 2:
        ups = [band]
    else:
        ups = [jnp.int32(1), jnp.int32(0)]
    built = [tables(up) for up in ups]
    table, own_mix, _ = built[0]
    weight_sent = regroup(weight_near, [own_mix], "regroup_weight")
    weight_far = [swap(weight_sent[x - 1], x * NEAR) for x in range(far - 1, 0, -1)]
    flux_sent = regroup(flux_far, [weight_sent[0]], "regroup_flux", backward=True)
    flux_near = [swap(part, y + 1) for y, part in enumerate(flux_sent)]

    edge_shape = shape((visits, ACROSS, HALO, LANES), BF16)
    edge_count = 1 if bands == 2 else 2
    frame, note, *edges = pl.pallas_call(
        functools.partial(place_kernel, far, bands == 2),
        out_shape=(shape((visits, ACROSS, ROWS, LANES), BF16), shape((TILE_ROWS, LANES), F32))
        + (edge_shape,) * edge_count,
        in_specs=[vmem()] * (far + NEAR - 1),
        out_specs=(vmem(),) * (2 + edge_count),
        compiler_params=params(),
        name="place_flux",
    )(*flux_far, *flux_near)

    if bands == 2:
        halos = [lax.ppermute(edges[0], "band", [(0, 1), (1, 0)])]
    else:
        down = [(i, i + 1) for i in range(bands - 1)]
        halos = [
            lax.ppermute(edges[1], "band", down),
            lax.ppermute(edges[0], "band", [(j, i) for i, j in down]),
        ]
    parts = [filter_rows(frame, table, own_mix, "filter_own")]
    for halo, (_, _, halo_mix) in zip(halos, built):
        parts.append(filter_rows(halo, table, halo_mix, "filter_halo"))
    return pl.pallas_call(
        functools.partial(final_kernel, far),
        out_shape=shape((1, ROWS, COLS), F32),
        in_specs=[vmem()] * (NEAR + far + len(parts)),
        out_specs=vmem(),
        compiler_params=params(),
        name="final",
    )(note, *weight_near, *weight_far, *parts)


def solution(mesh):
    in_specs = (
        P(None, ("patch", "band"), None, None),
        P(None, ("patch", "band"), None, None),
        P(None, ("patch", "band")),
        P(None, ("patch", "band")),
        P(),
        P("patch", None, None, None),
    )
    out_specs = P("patch", "band", None)
    return jax.shard_map(
        per_device, mesh=mesh, in_specs=in_specs, out_specs=out_specs, check_vma=False
    )
```

```python
import functools

import jax
import jax.numpy as jnp
from jax import lax
from jax.experimental import pallas as pl
from jax.experimental.pallas import tpu as pltpu
from jax.sharding import PartitionSpec as P

BASIS = 21
GROUPS = 24
TAPS = 31
MARGIN = TAPS // 2
ROWS = 32
COLS = 512
TILE_ROWS = 8
LANES = 128
ACROSS = COLS // LANES
DOWN = ROWS // TILE_ROWS
CAP = 2
NEAR = 4
HALO = 16
PAIR = 2 * LANES
F32 = jnp.float32
BF16 = jnp.bfloat16
I32 = jnp.int32


def iota(shape, dim):
    return lax.broadcasted_iota(I32, shape, dim)


def vmem():
    return pl.BlockSpec(memory_space=pltpu.VMEM)


def smem():
    return pl.BlockSpec(memory_space=pltpu.SMEM)


def hbm():
    return pl.BlockSpec(memory_space=pltpu.HBM)


def in_hbm(value):
    return pltpu.with_memory_space_constraint(value, pltpu.HBM)


def params():
    return pltpu.CompilerParams(vmem_limit_bytes=40 * 1024 * 1024)


def cost(flops, moved):
    return pl.CostEstimate(flops=flops, bytes_accessed=moved, transcendentals=0)


def slots_of(dest):
    count = dest.shape[1]
    lane = iota(dest.shape, 1)
    ordinal = jnp.zeros(dest.shape, I32)
    for t in range(count - 1):
        same = jnp.logical_and(dest == dest[:, t : t + 1], lane > t)
        ordinal = ordinal + jnp.where(same, 1, 0)
    return dest * CAP + ordinal


def spread(values, width, repeat):
    m = values.shape[1]
    hot = (iota((m, width), 1) // repeat == iota((m, width), 0)).astype(F32).astype(BF16)
    return jnp.dot(values.astype(F32).astype(BF16), hot, preferred_element_type=F32).astype(I32)


def start_copies(pairs, sems):
    copies = [pltpu.make_async_copy(src, dst, sems.at[i]) for i, (src, dst) in enumerate(pairs)]
    for copy in copies:
        copy.start()
    return copies


def sort_visit(goal, tiles, slots):
    row = iota((slots * TILE_ROWS, goal.shape[1]), 0)
    hot = jnp.where(row == goal, 1.0, 0.0).astype(BF16)
    return jnp.dot(hot, tiles, preferred_element_type=F32).astype(BF16)


def pack_kernel(far, dest_hbm, block_hbm, flux_hbm, weight_hbm, *refs):
    far_out, near_out = refs[: far - 1], refs[far - 1 : far - 1 + NEAR]
    landing, sems = refs[far - 1 + NEAR : -1], refs[-1]
    copies = start_copies(zip((dest_hbm, block_hbm, flux_hbm, weight_hbm), landing), sems)
    dest_ref, block_ref, flux_ref, weight_ref = landing
    visits, depth, _ = flux_ref.shape
    block = CAP * TILE_ROWS
    span = visits * block
    copies[0].wait()
    copies[1].wait()
    slot = slots_of(jnp.bitwise_xor(dest_ref[...], lax.axis_index("patch")))
    goal = spread(slot, depth, TILE_ROWS) * TILE_ROWS + iota((visits, depth), 1) % TILE_ROWS
    place = block_ref[...] % ACROSS * DOWN + block_ref[...] // ACROSS + 1
    lane = iota((TILE_ROWS, LANES), 1)
    for x in range(far):
        note = jnp.zeros((TILE_ROWS, LANES), F32)
        for y in range(NEAR):
            for o in range(CAP):
                chosen = slot == CAP * (x * NEAR + y) + o
                value = jnp.sum(jnp.where(chosen, place, 0).astype(F32), axis=1, keepdims=True)
                value = jnp.concatenate([value, jnp.zeros((TILE_ROWS - visits, 1), F32)], axis=0)
                note = jnp.where(lane == CAP * (y * far + x) + o, value, note)
        note = note.astype(BF16)
        if x:
            far_out[x - 1][NEAR * span :, :] = note
        else:
            for out in near_out:
                out[(far + 1) * span :, :] = note
    copies[2].wait()
    copies[3].wait()
    for k in range(visits):
        both = jnp.concatenate([flux_ref[k], weight_ref[k]], axis=1)
        moved = sort_visit(goal[k : k + 1], both, far * NEAR * CAP)
        for x in range(far):
            for y in range(NEAR):
                rel = x * NEAR + y
                part = moved[rel * block : (rel + 1) * block]
                if x:
                    far_out[x - 1][part_of(y, span, k, block), :] = part[:, :LANES]
                else:
                    near_out[y][part_of(far, span, k, block), :] = part[:, :LANES]
                near_out[y][part_of(x, span, k, block), :] = part[:, LANES:]


def part_of(i, span, k, block):
    return slice(i * span + k * block, i * span + (k + 1) * block)


def regroup_kernel(count, span, skip, *refs):
    ins = refs[:count]
    outs = refs[count + skip :]
    for j, out in enumerate(outs):
        for i, part in enumerate(ins):
            out[i * span : (i + 1) * span, :] = part[(j + 1) * span : (j + 2) * span, :]
        if out.shape[0] > count * span:
            tail = sum(part[part.shape[0] - TILE_ROWS :, :].astype(F32) for part in ins)
            out[count * span :, :] = tail.astype(BF16)


def placing(note, senders):
    width = senders * CAP * TILE_ROWS
    hot = (iota((LANES, width), 1) // TILE_ROWS == iota((LANES, width), 0)).astype(F32).astype(BF16)
    place = jnp.dot(note.astype(BF16), hot, preferred_element_type=F32).astype(I32) - 1
    return place * TILE_ROWS + iota((TILE_ROWS, width), 1) % TILE_ROWS


def place_kernel(far, swap, *refs):
    chunks, others = refs[: far - 1], refs[far - 1 : far + NEAR - 2]
    nears, (frame_ref, hot_ref, *edges) = refs[far + NEAR - 2 : far + 2 * NEAR - 2], refs[far + 2 * NEAR - 2 :]
    visits = frame_ref.shape[0]
    block = CAP * TILE_ROWS
    span = visits * block
    path = iota((TILE_ROWS, LANES), 1) // (CAP * far)
    note = jnp.zeros((TILE_ROWS, LANES), F32)
    for y in range(NEAR):
        tails = [nears[y]] + (list(chunks) if y == 0 else [others[y - 1]])
        tail = sum(ref[ref.shape[0] - TILE_ROWS :, :].astype(F32) for ref in tails)
        note = jnp.where(path == y, tail, note)
    goal = placing(note, far * NEAR)
    for k in range(visits):
        hot = jnp.where(iota((ACROSS * ROWS, goal.shape[1]), 0) == goal[k : k + 1], 1.0, 0.0).astype(BF16)
        hot_ref[k] = hot
        received = []
        for y in range(NEAR):
            received.append(nears[y][part_of(far, span, k, block), :])
            for x in range(1, far):
                if y:
                    received.append(others[y - 1][part_of(x - 1, span, k, block), :])
                else:
                    received.append(chunks[x - 1][part_of(0, span, k, block), :])
        frame = jnp.dot(hot, jnp.concatenate(received, axis=0), preferred_element_type=F32).astype(BF16)
        frame = frame.reshape(ACROSS, ROWS, LANES)
        frame_ref[k] = frame
        top, bottom = frame[:, :HALO], frame[:, ROWS - HALO :]
        if swap:
            edges[0][k] = jnp.where(lax.axis_index("band") == 0, bottom, top)
        else:
            edges[0][k] = top
            edges[1][k] = bottom


def hot_rows(taps, shift_lane, width, used=None):
    lane = iota((TAPS, width), 1)
    tap = iota((TAPS, width), 0)
    hot = lane == shift_lane(tap)
    if used is not None:
        hot = jnp.logical_and(hot, used(tap))
    hot = hot.astype(F32).astype(BF16)
    return jnp.dot(taps, hot, preferred_element_type=F32)


def table_kernel(bands, up_ref, taps_hbm, spatial_hbm, table_ref, own_ref, halo_ref, taps_ref, spatial_ref, sems):
    copies = start_copies(((taps_hbm, taps_ref), (spatial_hbm, spatial_ref)), sems)
    for copy in copies:
        copy.wait()
    taps = [taps_ref[b].astype(F32) for b in range(BASIS)]
    blank = [jnp.zeros((GROUPS - BASIS, TAPS), F32)]
    column, line_taps = (
        jnp.concatenate([tap[i : i + 1] for tap in taps] + blank, axis=0).astype(BF16) for i in range(2)
    )
    low = LANES // 2 - MARGIN
    lines = hot_rows(column, lambda tap: (-low - tap) % LANES, LANES)
    gap = iota((PAIR, LANES), 0) - iota((PAIR, LANES), 1) - low
    inside = jnp.logical_and(gap >= 0, gap < TAPS)
    for b in range(table_ref.shape[1] // LANES):
        if b < BASIS:
            line = jnp.broadcast_to(lines[b : b + 1], (PAIR, LANES))
            rolled = pltpu.roll(line, 0, 1, stride=1, stride_axis=0)
            part = jnp.where(inside, rolled, 0.0)
        else:
            part = jnp.zeros((PAIR, LANES), F32)
        table_ref[:, b * LANES : (b + 1) * LANES] = part.astype(BF16)

    visits = own_ref.shape[0]
    row = lax.axis_index("band") * ROWS + iota((ROWS, LANES), 0)
    coord = (2.0 * row.astype(F32) + 1.0) / (ROWS * bands) - 1.0
    spatial = jnp.concatenate([spatial_ref[i] for i in range(3 * visits)], axis=0)

    def fill(out_ref, height, offset, used=None):
        fit = LANES // height
        line = 0.0
        which = iota((GROUPS, LANES), 0)
        for j in range(fit):
            part = hot_rows(
                line_taps, lambda tap: (height * j + tap - offset + 2 * LANES) % LANES, LANES, used
            )
            line = line + jnp.where(which % fit == j, part, 0.0)
        t = iota((ROWS, LANES), 1) % height
        tap = t - iota((ROWS, LANES), 0) + offset
        good = jnp.logical_and(tap >= 0, tap < TAPS)
        width = GROUPS * height
        hot = (iota((BASIS, width), 1) // height == iota((BASIS, width), 0)).astype(F32)
        coef = jnp.dot(spatial, hot, precision=lax.Precision.HIGHEST, preferred_element_type=F32)
        for g in range(GROUPS // fit):
            here = jnp.sum(line[g * fit : (g + 1) * fit], axis=0, keepdims=True)
            rolled = pltpu.roll(jnp.broadcast_to(here, (ROWS, LANES)), 0, 1, stride=1, stride_axis=0)
            taps = jnp.where(good, rolled, 0.0)
            lanes = slice(g * LANES, (g + 1) * LANES)
            for k in range(visits):
                c = coef[3 * k : 3 * k + 3, lanes]
                out_ref[k, :ROWS, lanes] = ((c[0:1] + coord * c[1:2]) * taps).astype(BF16)
                out_ref[k, ROWS:, lanes] = (c[2:3] * taps).astype(BF16)

    fill(own_ref, ROWS, MARGIN)
    up = up_ref[0] > 0
    low = jnp.where(up, 0, MARGIN + 1)
    fill(
        halo_ref,
        HALO,
        jnp.where(up, MARGIN - HALO, MARGIN + ROWS),
        lambda tap: jnp.logical_and(tap >= low, tap < low + MARGIN),
    )


def filter_kernel(frame_ref, table_ref, mix_ref, *refs):
    before, (out_ref, windows, filtered) = refs[:-3], refs[-3:]
    visits, _, height, _ = frame_ref.shape
    half = LANES // 2
    left = iota((height, LANES), 1) < half
    count = ACROSS * height
    for k in range(visits):
        rolled = [pltpu.roll(frame_ref[k, c].astype(F32), half, 1) for c in range(ACROSS)]
        zero = jnp.zeros((height, LANES), F32)
        padded = [zero] + rolled + [zero]
        pieces = [jnp.where(left, padded[c], padded[c + 1]).astype(BF16) for c in range(ACROSS + 1)]
        for c in range(ACROSS):
            rows = slice(k * count + c * height, k * count + (c + 1) * height)
            windows[rows, :LANES] = pieces[c]
            windows[rows, LANES:] = pieces[c + 1]
    done = table_ref.shape[1] // LANES
    filtered[:, done * height :, :] = jnp.zeros((visits, filtered.shape[1] - done * height, COLS), BF16)
    for p in range(done // 2):
        part = jnp.dot(windows[...], table_ref[:, p * PAIR : (p + 1) * PAIR], preferred_element_type=F32).astype(BF16)
        for k in range(visits):
            for c in range(ACROSS):
                for j in range(2):
                    b = 2 * p + j
                    filtered[k, b * height : (b + 1) * height, c * LANES : (c + 1) * LANES] = part[
                        k * count + c * height : k * count + (c + 1) * height, j * LANES : (j + 1) * LANES
                    ]
    col = (2.0 * iota((1, COLS), 1).astype(F32) + 1.0) / COLS - 1.0
    for k in range(visits):
        both = jnp.dot(mix_ref[k], filtered[k], preferred_element_type=F32)
        out_ref[k] = sum((part[k] for part in before), both[:ROWS] + col * both[ROWS:])


def final_kernel(order, hot_ref, *refs):
    nears, fars = refs[:NEAR], dict(zip(order, refs[NEAR:]))
    value_ref, out_ref = refs[-2:]
    block = CAP * TILE_ROWS
    visits = hot_ref.shape[0]
    span = visits * block
    total = jnp.zeros((ACROSS * ROWS, LANES), F32)
    sums = [jnp.zeros((ROWS, LANES), F32) for _ in range(ACROSS)]
    for k in range(visits):
        received = []
        for y in range(NEAR):
            received.append(nears[y][part_of(0, span, k, block), :])
            received += [fars[x][part_of(y, span, k, block), :] for x in sorted(order)]
        weight = jnp.dot(hot_ref[k], jnp.concatenate(received, axis=0), preferred_element_type=F32)
        total = total + weight
        for c in range(ACROSS):
            value = value_ref[k, :, c * LANES : (c + 1) * LANES]
            sums[c] = sums[c] + weight[c * ROWS : (c + 1) * ROWS] * value
    for c in range(ACROSS):
        out_ref[0, :, c * LANES : (c + 1) * LANES] = sums[c] / total[c * ROWS : (c + 1) * ROWS]


def shape(dims, kind):
    return jax.ShapeDtypeStruct(dims, kind)


def filter_rows(frame, table, mix, before, name):
    visits, _, height, _ = frame.shape
    return pl.pallas_call(
        filter_kernel,
        out_shape=shape((visits, ROWS, COLS), F32),
        in_specs=[vmem()] * (3 + len(before)),
        out_specs=vmem(),
        scratch_shapes=[
            pltpu.VMEM((visits * ACROSS * height, PAIR), BF16),
            pltpu.VMEM((visits, GROUPS * height, COLS), BF16),
        ],
        compiler_params=params(),
        cost_estimate=cost(4 * visits * ACROSS * height * PAIR * BASIS * LANES, 4 * 1024 * 1024),
        name=name,
    )(frame, table, mix, *before)


def regroup(parts, count, span, tail, after, name):
    rows = len(parts) * span + (TILE_ROWS if tail else 0)
    return pl.pallas_call(
        functools.partial(regroup_kernel, len(parts), span, len(after)),
        out_shape=(shape((rows, LANES), BF16),) * (count - 1),
        in_specs=[vmem()] * len(parts) + [pl.BlockSpec(memory_space=pl.ANY)] * len(after),
        out_specs=(vmem(),) * (count - 1),
        compiler_params=params(),
        name=name,
    )(*parts, *after)


def per_device(tile_flux, tile_weight, dest_patch, dest_block, basis, spatial):
    visits, tile_count, tile_height, tile_width = tile_flux.shape
    patches, bands = lax.axis_size("patch"), lax.axis_size("band")
    band = lax.axis_index("band")
    far = patches // NEAR
    depth = tile_count * tile_height
    block = CAP * TILE_ROWS
    flux = tile_flux.reshape(visits, depth, tile_width)
    weight = tile_weight.reshape(visits, depth, tile_width)

    def swap(value, step):
        return lax.ppermute(value, "patch", [(i, i ^ step) for i in range(patches)])

    span = visits * block
    fars = range(1, far)
    packed = pl.pallas_call(
        functools.partial(pack_kernel, far),
        out_shape=(shape((NEAR * span + TILE_ROWS, LANES), BF16),) * (far - 1)
        + (shape(((far + 1) * span + TILE_ROWS, LANES), BF16),) * NEAR,
        in_specs=[hbm()] * 4,
        out_specs=(vmem(),) * (far - 1 + NEAR),
        scratch_shapes=[
            pltpu.VMEM(dest_patch.shape, I32),
            pltpu.VMEM(dest_block.shape, I32),
            pltpu.VMEM(flux.shape, BF16),
            pltpu.VMEM(weight.shape, BF16),
            pltpu.SemaphoreType.DMA((4,)),
        ],
        compiler_params=params(),
        name="pack",
    )(*map(in_hbm, (dest_patch, dest_block, flux, weight)))
    chunks = [swap(packed[x - 1], x * NEAR) for x in fars]
    nears = [packed[far - 1]] + [swap(packed[far - 1 + y], y) for y in range(1, NEAR)]

    coefs = spatial.reshape(visits * 3, 1, BASIS)
    taps = basis.transpose(1, 0, 2)

    def tables(up):
        return pl.pallas_call(
            functools.partial(table_kernel, bands),
            out_shape=(
                shape((PAIR, 2 * pl.cdiv(BASIS, 2) * LANES), BF16),
                shape((visits, 2 * ROWS, GROUPS * ROWS), BF16),
                shape((visits, 2 * ROWS, GROUPS * HALO), BF16),
            ),
            in_specs=[smem()] + [hbm()] * 2,
            out_specs=(vmem(),) * 3,
            scratch_shapes=[
                pltpu.VMEM(taps.shape, BF16),
                pltpu.VMEM(coefs.shape, F32),
                pltpu.SemaphoreType.DMA((2,)),
            ],
            compiler_params=params(),
            cost_estimate=cost(10**9, 4 * 1024 * 1024),
            name="tables",
        )(up.reshape(1).astype(I32), in_hbm(taps), in_hbm(coefs))

    if bands == 2:
        ups = [band]
    else:
        ups = [jnp.int32(1), jnp.int32(0)]
    built = [tables(up) for up in ups]
    table, own_mix, _ = built[0]
    flux_sent = regroup(chunks, NEAR, span, True, [own_mix], "regroup_flux")
    others = [swap(flux_sent[y - 1], y) for y in range(1, NEAR)]
    weight_sent = regroup(nears, far, span, False, [flux_sent[0]], "regroup_weight")
    order = sorted(fars, key=lambda x: (x != far // 2, x != 1, -x))
    weights = [swap(weight_sent[x - 1], x * NEAR) for x in order]

    edge_shape = shape((visits, ACROSS, HALO, LANES), BF16)
    edge_count = 1 if bands == 2 else 2
    frame, hot, *edges = pl.pallas_call(
        functools.partial(place_kernel, far, bands == 2),
        out_shape=(
            shape((visits, ACROSS, ROWS, LANES), BF16),
            shape((visits, ACROSS * ROWS, patches * block), BF16),
        )
        + (edge_shape,) * edge_count,
        in_specs=[vmem()] * (far + 2 * NEAR - 2),
        out_specs=(vmem(),) * (2 + edge_count),
        compiler_params=params(),
        name="place_flux",
    )(*chunks, *others, *nears)

    if bands == 2:
        halos = [lax.ppermute(edges[0], "band", [(0, 1), (1, 0)])]
    else:
        down = [(i, i + 1) for i in range(bands - 1)]
        halos = [
            lax.ppermute(edges[1], "band", down),
            lax.ppermute(edges[0], "band", [(j, i) for i, j in down]),
        ]
    value = filter_rows(frame, table, own_mix, [], "filter_own")
    for halo, (_, _, halo_mix) in zip(halos, built):
        value = filter_rows(halo, table, halo_mix, [value], "filter_halo")
    return pl.pallas_call(
        functools.partial(final_kernel, order),
        out_shape=shape((1, ROWS, COLS), F32),
        in_specs=[vmem()] * (1 + NEAR + far),
        out_specs=vmem(),
        compiler_params=params(),
        name="final",
    )(hot, *nears, *weights, value)


def solution(mesh):
    in_specs = (
        P(None, ("patch", "band"), None, None),
        P(None, ("patch", "band"), None, None),
        P(None, ("patch", "band")),
        P(None, ("patch", "band")),
        P(),
        P("patch", None, None, None),
    )
    out_specs = P("patch", "band", None)
    return jax.shard_map(
        per_device, mesh=mesh, in_specs=in_specs, out_specs=out_specs, check_vma=False
    )
```

```python
import functools

import jax
import jax.numpy as jnp
from jax import lax
from jax.experimental import pallas as pl
from jax.experimental.pallas import tpu as pltpu
from jax.sharding import PartitionSpec as P

BASIS = 21
GROUPS = 24
TAPS = 31
MARGIN = TAPS // 2
ROWS = 32
COLS = 512
TILE_ROWS = 8
LANES = 128
ACROSS = COLS // LANES
DOWN = ROWS // TILE_ROWS
CAP = 2
NEAR = 4
HALO = 16
PAIR = 2 * LANES
F32 = jnp.float32
BF16 = jnp.bfloat16
I32 = jnp.int32


def iota(shape, dim):
    return lax.broadcasted_iota(I32, shape, dim)


def vmem():
    return pl.BlockSpec(memory_space=pltpu.VMEM)


def smem():
    return pl.BlockSpec(memory_space=pltpu.SMEM)


def hbm():
    return pl.BlockSpec(memory_space=pltpu.HBM)


def in_hbm(value):
    return pltpu.with_memory_space_constraint(value, pltpu.HBM)


def params():
    return pltpu.CompilerParams(vmem_limit_bytes=40 * 1024 * 1024)


def cost(flops, moved):
    return pl.CostEstimate(flops=flops, bytes_accessed=moved, transcendentals=0)


def slots_of(dest):
    count = dest.shape[1]
    lane = iota(dest.shape, 1)
    ordinal = jnp.zeros(dest.shape, I32)
    for t in range(count - 1):
        same = jnp.logical_and(dest == dest[:, t : t + 1], lane > t)
        ordinal = ordinal + jnp.where(same, 1, 0)
    return dest * CAP + ordinal


def spread(values, width, repeat):
    m = values.shape[1]
    hot = (iota((m, width), 1) // repeat == iota((m, width), 0)).astype(F32).astype(BF16)
    return jnp.dot(values.astype(F32).astype(BF16), hot, preferred_element_type=F32).astype(I32)


def start_copies(pairs, sems):
    copies = [pltpu.make_async_copy(src, dst, sems.at[i]) for i, (src, dst) in enumerate(pairs)]
    for copy in copies:
        copy.start()
    return copies


def sort_visit(goal, tiles, slots):
    row = iota((slots * TILE_ROWS, goal.shape[1]), 0)
    hot = jnp.where(row == goal, 1.0, 0.0).astype(BF16)
    return jnp.dot(hot, tiles, preferred_element_type=F32).astype(BF16)


def pack_kernel(far, dest_hbm, block_hbm, flux_hbm, weight_hbm, *refs):
    far_out, near_out = refs[: far - 1], refs[far - 1 : far - 1 + NEAR]
    landing, sems = refs[far - 1 + NEAR : -1], refs[-1]
    copies = start_copies(zip((dest_hbm, block_hbm, flux_hbm, weight_hbm), landing), sems)
    dest_ref, block_ref, flux_ref, weight_ref = landing
    visits, depth, _ = flux_ref.shape
    block = CAP * TILE_ROWS
    span = visits * block
    copies[0].wait()
    copies[1].wait()
    slot = slots_of(jnp.bitwise_xor(dest_ref[...], lax.axis_index("patch")))
    goal = spread(slot, depth, TILE_ROWS) * TILE_ROWS + iota((visits, depth), 1) % TILE_ROWS
    place = block_ref[...] % ACROSS * DOWN + block_ref[...] // ACROSS + 1
    lane = iota((TILE_ROWS, LANES), 1)
    for x in range(far):
        note = jnp.zeros((TILE_ROWS, LANES), F32)
        for y in range(NEAR):
            for o in range(CAP):
                chosen = slot == CAP * (x * NEAR + y) + o
                value = jnp.sum(jnp.where(chosen, place, 0).astype(F32), axis=1, keepdims=True)
                value = jnp.concatenate([value, jnp.zeros((TILE_ROWS - visits, 1), F32)], axis=0)
                note = jnp.where(lane == CAP * (y * far + x) + o, value, note)
        note = note.astype(BF16)
        if x:
            far_out[x - 1][NEAR * span :, :] = note
        else:
            for out in near_out:
                out[(far + 1) * span :, :] = note
    copies[2].wait()
    copies[3].wait()
    for k in range(visits):
        both = jnp.concatenate([flux_ref[k], weight_ref[k]], axis=1)
        moved = sort_visit(goal[k : k + 1], both, far * NEAR * CAP)
        for x in range(far):
            for y in range(NEAR):
                rel = x * NEAR + y
                part = moved[rel * block : (rel + 1) * block]
                if x:
                    far_out[x - 1][part_of(y, span, k, block), :] = part[:, :LANES]
                else:
                    near_out[y][part_of(far, span, k, block), :] = part[:, :LANES]
                near_out[y][part_of(x, span, k, block), :] = part[:, LANES:]


def part_of(i, span, k, block):
    return slice(i * span + k * block, i * span + (k + 1) * block)


def sorted_refs(order, refs):
    return [ref for _, ref in sorted(zip(order, refs), key=lambda pair: pair[0])]


def regroup_kernel(order, span, skip, *refs):
    count = len(order)
    ins = sorted_refs(order, refs)
    outs = refs[count + skip :]
    for j, out in enumerate(outs):
        for i, part in enumerate(ins):
            out[i * span : (i + 1) * span, :] = part[(j + 1) * span : (j + 2) * span, :]
        if out.shape[0] > count * span:
            tail = sum(part[part.shape[0] - TILE_ROWS :, :].astype(F32) for part in ins)
            out[count * span :, :] = tail.astype(BF16)


def placing(note, senders):
    width = senders * CAP * TILE_ROWS
    hot = (iota((LANES, width), 1) // TILE_ROWS == iota((LANES, width), 0)).astype(F32).astype(BF16)
    place = jnp.dot(note.astype(BF16), hot, preferred_element_type=F32).astype(I32) - 1
    return place * TILE_ROWS + iota((TILE_ROWS, width), 1) % TILE_ROWS


def place_kernel(far, order, swap, *refs):
    chunks, others = sorted_refs(order, refs[: far - 1]), refs[far - 1 : far + NEAR - 2]
    nears, (frame_ref, hot_ref, *edges) = refs[far + NEAR - 2 : far + 2 * NEAR - 2], refs[far + 2 * NEAR - 2 :]
    visits = frame_ref.shape[0]
    block = CAP * TILE_ROWS
    span = visits * block
    path = iota((TILE_ROWS, LANES), 1) // (CAP * far)
    note = jnp.zeros((TILE_ROWS, LANES), F32)
    for y in range(NEAR):
        tails = [nears[y]] + (list(chunks) if y == 0 else [others[y - 1]])
        tail = sum(ref[ref.shape[0] - TILE_ROWS :, :].astype(F32) for ref in tails)
        note = jnp.where(path == y, tail, note)
    goal = placing(note, far * NEAR)
    for k in range(visits):
        hot = jnp.where(iota((ACROSS * ROWS, goal.shape[1]), 0) == goal[k : k + 1], 1.0, 0.0).astype(BF16)
        hot_ref[k] = hot
        received = []
        for y in range(NEAR):
            received.append(nears[y][part_of(far, span, k, block), :])
            for x in range(1, far):
                if y:
                    received.append(others[y - 1][part_of(x - 1, span, k, block), :])
                else:
                    received.append(chunks[x - 1][part_of(0, span, k, block), :])
        frame = jnp.dot(hot, jnp.concatenate(received, axis=0), preferred_element_type=F32).astype(BF16)
        frame = frame.reshape(ACROSS, ROWS, LANES)
        frame_ref[k] = frame
        top, bottom = frame[:, :HALO], frame[:, ROWS - HALO :]
        if swap:
            edges[0][k] = jnp.where(lax.axis_index("band") == 0, bottom, top)
        else:
            edges[0][k] = top
            edges[1][k] = bottom


def hot_rows(taps, shift_lane, width, used=None):
    lane = iota((TAPS, width), 1)
    tap = iota((TAPS, width), 0)
    hot = lane == shift_lane(tap)
    if used is not None:
        hot = jnp.logical_and(hot, used(tap))
    hot = hot.astype(F32).astype(BF16)
    return jnp.dot(taps, hot, preferred_element_type=F32)


def table_kernel(bands, up_ref, taps_hbm, spatial_hbm, table_ref, own_ref, halo_ref, taps_ref, spatial_ref, sems):
    copies = start_copies(((taps_hbm, taps_ref), (spatial_hbm, spatial_ref)), sems)
    for copy in copies:
        copy.wait()
    taps = [taps_ref[b].astype(F32) for b in range(BASIS)]
    blank = [jnp.zeros((GROUPS - BASIS, TAPS), F32)]
    column, line_taps = (
        jnp.concatenate([tap[i : i + 1] for tap in taps] + blank, axis=0).astype(BF16) for i in range(2)
    )
    low = LANES // 2 - MARGIN
    lines = hot_rows(column, lambda tap: (-low - tap) % LANES, LANES)
    gap = iota((PAIR, LANES), 0) - iota((PAIR, LANES), 1) - low
    inside = jnp.logical_and(gap >= 0, gap < TAPS)
    for b in range(table_ref.shape[1] // LANES):
        if b < BASIS:
            line = jnp.broadcast_to(lines[b : b + 1], (PAIR, LANES))
            rolled = pltpu.roll(line, 0, 1, stride=1, stride_axis=0)
            part = jnp.where(inside, rolled, 0.0)
        else:
            part = jnp.zeros((PAIR, LANES), F32)
        table_ref[:, b * LANES : (b + 1) * LANES] = part.astype(BF16)

    visits = own_ref.shape[0]
    row = lax.axis_index("band") * ROWS + iota((ROWS, LANES), 0)
    coord = (2.0 * row.astype(F32) + 1.0) / (ROWS * bands) - 1.0
    spatial = jnp.concatenate([spatial_ref[i] for i in range(3 * visits)], axis=0)

    def fill(out_ref, height, offset, used=None):
        fit = LANES // height
        line = 0.0
        which = iota((GROUPS, LANES), 0)
        for j in range(fit):
            part = hot_rows(
                line_taps, lambda tap: (height * j + tap - offset + 2 * LANES) % LANES, LANES, used
            )
            line = line + jnp.where(which % fit == j, part, 0.0)
        t = iota((ROWS, LANES), 1) % height
        tap = t - iota((ROWS, LANES), 0) + offset
        good = jnp.logical_and(tap >= 0, tap < TAPS)
        width = GROUPS * height
        hot = (iota((BASIS, width), 1) // height == iota((BASIS, width), 0)).astype(F32)
        coef = jnp.dot(spatial, hot, precision=lax.Precision.HIGHEST, preferred_element_type=F32)
        for g in range(GROUPS // fit):
            here = jnp.sum(line[g * fit : (g + 1) * fit], axis=0, keepdims=True)
            rolled = pltpu.roll(jnp.broadcast_to(here, (ROWS, LANES)), 0, 1, stride=1, stride_axis=0)
            taps = jnp.where(good, rolled, 0.0)
            lanes = slice(g * LANES, (g + 1) * LANES)
            for k in range(visits):
                c = coef[3 * k : 3 * k + 3, lanes]
                out_ref[k, :ROWS, lanes] = ((c[0:1] + coord * c[1:2]) * taps).astype(BF16)
                out_ref[k, ROWS:, lanes] = (c[2:3] * taps).astype(BF16)

    fill(own_ref, ROWS, MARGIN)
    up = up_ref[0] > 0
    low = jnp.where(up, 0, MARGIN + 1)
    fill(
        halo_ref,
        HALO,
        jnp.where(up, MARGIN - HALO, MARGIN + ROWS),
        lambda tap: jnp.logical_and(tap >= low, tap < low + MARGIN),
    )


def filter_kernel(order, frame_ref, table_ref, mix_ref, *refs):
    (*others, out_ref, windows, filtered) = refs
    weighing = []
    if order:
        count = 1 + NEAR + len(order)
        others, weighing = others[:-count], others[-count:]
    visits, _, height, _ = frame_ref.shape
    half = LANES // 2
    left = iota((height, LANES), 1) < half
    count = ACROSS * height
    for k in range(visits):
        rolled = [pltpu.roll(frame_ref[k, c].astype(F32), half, 1) for c in range(ACROSS)]
        zero = jnp.zeros((height, LANES), F32)
        padded = [zero] + rolled + [zero]
        pieces = [jnp.where(left, padded[c], padded[c + 1]).astype(BF16) for c in range(ACROSS + 1)]
        for c in range(ACROSS):
            rows = slice(k * count + c * height, k * count + (c + 1) * height)
            windows[rows, :LANES] = pieces[c]
            windows[rows, LANES:] = pieces[c + 1]
    done = table_ref.shape[1] // LANES
    filtered[:, done * height :, :] = jnp.zeros((visits, filtered.shape[1] - done * height, COLS), BF16)
    for p in range(done // 2):
        part = jnp.dot(windows[...], table_ref[:, p * PAIR : (p + 1) * PAIR], preferred_element_type=F32).astype(BF16)
        for k in range(visits):
            for c in range(ACROSS):
                for j in range(2):
                    b = 2 * p + j
                    filtered[k, b * height : (b + 1) * height, c * LANES : (c + 1) * LANES] = part[
                        k * count + c * height : k * count + (c + 1) * height, j * LANES : (j + 1) * LANES
                    ]
    col = (2.0 * iota((1, COLS), 1).astype(F32) + 1.0) / COLS - 1.0
    total, sums = 0.0, [0.0] * ACROSS
    for k in range(visits):
        both = jnp.dot(mix_ref[k], filtered[k], preferred_element_type=F32)
        value = sum((part[k] for part in others), both[:ROWS] + col * both[ROWS:])
        if order:
            weight = weight_of(k, order, *weighing)
            total = total + weight
            for c in range(ACROSS):
                part = value[:, c * LANES : (c + 1) * LANES]
                sums[c] = sums[c] + weight[c * ROWS : (c + 1) * ROWS] * part
        else:
            out_ref[k] = value
    if order:
        for c in range(ACROSS):
            out_ref[0, :, c * LANES : (c + 1) * LANES] = sums[c] / total[c * ROWS : (c + 1) * ROWS]


def weight_of(k, order, hot_ref, *refs):
    nears, fars = refs[:NEAR], sorted_refs(order, refs[NEAR:])
    block = CAP * TILE_ROWS
    span = hot_ref.shape[0] * block
    received = []
    for y in range(NEAR):
        received.append(nears[y][part_of(0, span, k, block), :])
        received += [ref[part_of(y, span, k, block), :] for ref in fars]
    return jnp.dot(hot_ref[k], jnp.concatenate(received, axis=0), preferred_element_type=F32)


def shape(dims, kind):
    return jax.ShapeDtypeStruct(dims, kind)


def filter_rows(frame, table, mix, before, name, order=(), weighing=()):
    visits, _, height, _ = frame.shape
    return pl.pallas_call(
        functools.partial(filter_kernel, order),
        out_shape=shape((1 if order else visits, ROWS, COLS), F32),
        in_specs=[vmem()] * (3 + len(before) + len(weighing)),
        out_specs=vmem(),
        scratch_shapes=[
            pltpu.VMEM((visits * ACROSS * height, PAIR), BF16),
            pltpu.VMEM((visits, GROUPS * height, COLS), BF16),
        ],
        compiler_params=params(),
        cost_estimate=cost(4 * visits * ACROSS * height * PAIR * BASIS * LANES, 4 * 1024 * 1024),
        name=name,
    )(frame, table, mix, *before, *weighing)


def regroup(parts, order, count, span, tail, after, name):
    rows = len(parts) * span + (TILE_ROWS if tail else 0)
    return pl.pallas_call(
        functools.partial(regroup_kernel, order, span, len(after)),
        out_shape=(shape((rows, LANES), BF16),) * (count - 1),
        in_specs=[vmem()] * len(parts) + [pl.BlockSpec(memory_space=pl.ANY)] * len(after),
        out_specs=(vmem(),) * (count - 1),
        compiler_params=params(),
        name=name,
    )(*parts, *after)


def per_device(tile_flux, tile_weight, dest_patch, dest_block, basis, spatial):
    visits, tile_count, tile_height, tile_width = tile_flux.shape
    patches, bands = lax.axis_size("patch"), lax.axis_size("band")
    band = lax.axis_index("band")
    far = patches // NEAR
    depth = tile_count * tile_height
    block = CAP * TILE_ROWS
    flux = tile_flux.reshape(visits, depth, tile_width)
    weight = tile_weight.reshape(visits, depth, tile_width)

    def swap(value, step):
        return lax.ppermute(value, "patch", [(i, i ^ step) for i in range(patches)])

    span = visits * block
    fars = range(1, far)
    packed = pl.pallas_call(
        functools.partial(pack_kernel, far),
        out_shape=(shape((NEAR * span + TILE_ROWS, LANES), BF16),) * (far - 1)
        + (shape(((far + 1) * span + TILE_ROWS, LANES), BF16),) * NEAR,
        in_specs=[hbm()] * 4,
        out_specs=(vmem(),) * (far - 1 + NEAR),
        scratch_shapes=[
            pltpu.VMEM(dest_patch.shape, I32),
            pltpu.VMEM(dest_block.shape, I32),
            pltpu.VMEM(flux.shape, BF16),
            pltpu.VMEM(weight.shape, BF16),
            pltpu.SemaphoreType.DMA((4,)),
        ],
        compiler_params=params(),
        name="pack",
    )(*map(in_hbm, (dest_patch, dest_block, flux, weight)))
    first = sorted(fars, key=lambda x: (x != far - 1, x))
    chunks = [swap(packed[x - 1], x * NEAR) for x in first]
    nears = [packed[far - 1]] + [swap(packed[far - 1 + y], y) for y in range(1, NEAR)]

    coefs = spatial.reshape(visits * 3, 1, BASIS)
    taps = basis.transpose(1, 0, 2)

    def tables(up):
        return pl.pallas_call(
            functools.partial(table_kernel, bands),
            out_shape=(
                shape((PAIR, 2 * pl.cdiv(BASIS, 2) * LANES), BF16),
                shape((visits, 2 * ROWS, GROUPS * ROWS), BF16),
                shape((visits, 2 * ROWS, GROUPS * HALO), BF16),
            ),
            in_specs=[smem()] + [hbm()] * 2,
            out_specs=(vmem(),) * 3,
            scratch_shapes=[
                pltpu.VMEM(taps.shape, BF16),
                pltpu.VMEM(coefs.shape, F32),
                pltpu.SemaphoreType.DMA((2,)),
            ],
            compiler_params=params(),
            cost_estimate=cost(10**9, 4 * 1024 * 1024),
            name="tables",
        )(up.reshape(1).astype(I32), in_hbm(taps), in_hbm(coefs))

    if bands == 2:
        ups = [band]
    else:
        ups = [jnp.int32(1), jnp.int32(0)]
    built = [tables(up) for up in ups]
    table, own_mix, _ = built[0]
    flux_sent = regroup(chunks, first, NEAR, span, True, [own_mix], "regroup_flux")
    others = [swap(flux_sent[y - 1], y) for y in range(1, NEAR)]
    weight_sent = regroup(nears, list(range(NEAR)), far, span, False, [flux_sent[0]], "regroup_weight")
    order = sorted(fars, key=lambda x: (x != far // 2, x != 1, -x))
    weights = [swap(weight_sent[x - 1], x * NEAR) for x in order]

    edge_shape = shape((visits, ACROSS, HALO, LANES), BF16)
    edge_count = 1 if bands == 2 else 2
    frame, hot, *edges = pl.pallas_call(
        functools.partial(place_kernel, far, first, bands == 2),
        out_shape=(
            shape((visits, ACROSS, ROWS, LANES), BF16),
            shape((visits, ACROSS * ROWS, patches * block), BF16),
        )
        + (edge_shape,) * edge_count,
        in_specs=[vmem()] * (far + 2 * NEAR - 2),
        out_specs=(vmem(),) * (2 + edge_count),
        compiler_params=params(),
        name="place_flux",
    )(*chunks, *others, *nears)

    if bands == 2:
        halos = [lax.ppermute(edges[0], "band", [(0, 1), (1, 0)])]
    else:
        down = [(i, i + 1) for i in range(bands - 1)]
        halos = [
            lax.ppermute(edges[1], "band", down),
            lax.ppermute(edges[0], "band", [(j, i) for i, j in down]),
        ]
    value = filter_rows(frame, table, own_mix, [], "filter_own")
    for halo, (_, _, halo_mix) in zip(halos[:-1], built):
        value = filter_rows(halo, table, halo_mix, [value], "filter_halo")
    weighing = (hot, *nears, *weights)
    return filter_rows(halos[-1], table, built[-1][2], [value], "filter_halo_weigh", order, weighing)


def solution(mesh):
    in_specs = (
        P(None, ("patch", "band"), None, None),
        P(None, ("patch", "band"), None, None),
        P(None, ("patch", "band")),
        P(None, ("patch", "band")),
        P(),
        P("patch", None, None, None),
    )
    out_specs = P("patch", "band", None)
    return jax.shard_map(
        per_device, mesh=mesh, in_specs=in_specs, out_specs=out_specs, check_vma=False
    )
```

```python
import functools

import jax
import jax.numpy as jnp
from jax import lax
from jax.experimental import pallas as pl
from jax.experimental.pallas import tpu as pltpu
from jax.sharding import PartitionSpec as P

BASIS = 21
GROUPS = 24
TAPS = 31
MARGIN = TAPS // 2
ROWS = 32
COLS = 512
TILE_ROWS = 8
LANES = 128
ACROSS = COLS // LANES
DOWN = ROWS // TILE_ROWS
CAP = 2
NEAR = 4
HALO = 16
PAIR = 2 * LANES
F32 = jnp.float32
BF16 = jnp.bfloat16
I32 = jnp.int32


def iota(shape, dim):
    return lax.broadcasted_iota(I32, shape, dim)


def vmem():
    return pl.BlockSpec(memory_space=pltpu.VMEM)


def smem():
    return pl.BlockSpec(memory_space=pltpu.SMEM)


def hbm():
    return pl.BlockSpec(memory_space=pltpu.HBM)


def in_hbm(value):
    return pltpu.with_memory_space_constraint(value, pltpu.HBM)


def params():
    return pltpu.CompilerParams(vmem_limit_bytes=40 * 1024 * 1024)


def cost(flops, moved):
    return pl.CostEstimate(flops=flops, bytes_accessed=moved, transcendentals=0)


def slots_of(dest):
    count = dest.shape[1]
    lane = iota(dest.shape, 1)
    ordinal = jnp.zeros(dest.shape, I32)
    for t in range(count - 1):
        same = jnp.logical_and(dest == dest[:, t : t + 1], lane > t)
        ordinal = ordinal + jnp.where(same, 1, 0)
    return dest * CAP + ordinal


def spread(values, width, repeat):
    m = values.shape[1]
    hot = (iota((m, width), 1) // repeat == iota((m, width), 0)).astype(F32).astype(BF16)
    return jnp.dot(values.astype(F32).astype(BF16), hot, preferred_element_type=F32).astype(I32)


def start_copies(pairs, sems):
    copies = [pltpu.make_async_copy(src, dst, sems.at[i]) for i, (src, dst) in enumerate(pairs)]
    for copy in copies:
        copy.start()
    return copies


def sort_visit(goal, tiles, slots):
    row = iota((slots * TILE_ROWS, goal.shape[1]), 0)
    hot = jnp.where(row == goal, 1.0, 0.0).astype(BF16)
    return jnp.dot(hot, tiles, preferred_element_type=F32).astype(BF16)


def pack_kernel(far, dest_hbm, block_hbm, flux_hbm, weight_hbm, *refs):
    far_out, near_out = refs[: far - 1], refs[far - 1 : far - 1 + NEAR]
    landing, sems = refs[far - 1 + NEAR : -1], refs[-1]
    copies = start_copies(zip((dest_hbm, block_hbm, flux_hbm, weight_hbm), landing), sems)
    dest_ref, block_ref, flux_ref, weight_ref = landing
    visits, depth, _ = flux_ref.shape
    block = CAP * TILE_ROWS
    span = visits * block
    copies[0].wait()
    copies[1].wait()
    dest, me = dest_ref[...], lax.axis_index("patch")
    across = (dest // NEAR - me // NEAR + far) % far
    slot = slots_of(across * NEAR + jnp.bitwise_xor(dest % NEAR, me % NEAR))
    goal = spread(slot, depth, TILE_ROWS) * TILE_ROWS + iota((visits, depth), 1) % TILE_ROWS
    place = block_ref[...] % ACROSS * DOWN + block_ref[...] // ACROSS + 1
    lane = iota((TILE_ROWS, LANES), 1)
    for x in range(far):
        note = jnp.zeros((TILE_ROWS, LANES), F32)
        for y in range(NEAR):
            for o in range(CAP):
                chosen = slot == CAP * (x * NEAR + y) + o
                value = jnp.sum(jnp.where(chosen, place, 0).astype(F32), axis=1, keepdims=True)
                value = jnp.concatenate([value, jnp.zeros((TILE_ROWS - visits, 1), F32)], axis=0)
                note = jnp.where(lane == CAP * (y * far + x) + o, value, note)
        note = note.astype(BF16)
        if x:
            far_out[x - 1][NEAR * span :, :] = note
        else:
            for out in near_out:
                out[(far + 1) * span :, :] = note
    copies[2].wait()
    copies[3].wait()
    for k in range(visits):
        both = jnp.concatenate([flux_ref[k], weight_ref[k]], axis=1)
        moved = sort_visit(goal[k : k + 1], both, far * NEAR * CAP)
        for x in range(far):
            for y in range(NEAR):
                rel = x * NEAR + y
                part = moved[rel * block : (rel + 1) * block]
                if x:
                    far_out[x - 1][part_of(y, span, k, block), :] = part[:, :LANES]
                else:
                    near_out[y][part_of(far, span, k, block), :] = part[:, :LANES]
                near_out[y][part_of(x, span, k, block), :] = part[:, LANES:]


def part_of(i, span, k, block):
    return slice(i * span + k * block, i * span + (k + 1) * block)


def sorted_refs(order, refs):
    return [ref for _, ref in sorted(zip(order, refs), key=lambda pair: pair[0])]


def regroup_kernel(order, span, skip, *refs):
    count = len(order)
    ins = sorted_refs(order, refs)
    outs = refs[count + skip :]
    for j, out in enumerate(outs):
        for i, part in enumerate(ins):
            out[i * span : (i + 1) * span, :] = part[(j + 1) * span : (j + 2) * span, :]
        if out.shape[0] > count * span:
            tail = sum(part[part.shape[0] - TILE_ROWS :, :].astype(F32) for part in ins)
            out[count * span :, :] = tail.astype(BF16)


def placing(note, senders):
    width = senders * CAP * TILE_ROWS
    hot = (iota((LANES, width), 1) // TILE_ROWS == iota((LANES, width), 0)).astype(F32).astype(BF16)
    place = jnp.dot(note.astype(BF16), hot, preferred_element_type=F32).astype(I32) - 1
    return place * TILE_ROWS + iota((TILE_ROWS, width), 1) % TILE_ROWS


def place_kernel(far, order, swap, *refs):
    chunks, others = sorted_refs(order, refs[: far - 1]), refs[far - 1 : far + NEAR - 2]
    nears, (frame_ref, hot_ref, *edges) = refs[far + NEAR - 2 : far + 2 * NEAR - 2], refs[far + 2 * NEAR - 2 :]
    visits = frame_ref.shape[0]
    block = CAP * TILE_ROWS
    span = visits * block
    path = iota((TILE_ROWS, LANES), 1) // (CAP * far)
    note = jnp.zeros((TILE_ROWS, LANES), F32)
    for y in range(NEAR):
        tails = [nears[y]] + (list(chunks) if y == 0 else [others[y - 1]])
        tail = sum(ref[ref.shape[0] - TILE_ROWS :, :].astype(F32) for ref in tails)
        note = jnp.where(path == y, tail, note)
    goal = placing(note, far * NEAR)
    for k in range(visits):
        hot = jnp.where(iota((ACROSS * ROWS, goal.shape[1]), 0) == goal[k : k + 1], 1.0, 0.0).astype(BF16)
        hot_ref[k] = hot
        received = []
        for y in range(NEAR):
            received.append(nears[y][part_of(far, span, k, block), :])
            for x in range(1, far):
                if y:
                    received.append(others[y - 1][part_of(x - 1, span, k, block), :])
                else:
                    received.append(chunks[x - 1][part_of(0, span, k, block), :])
        frame = jnp.dot(hot, jnp.concatenate(received, axis=0), preferred_element_type=F32).astype(BF16)
        frame = frame.reshape(ACROSS, ROWS, LANES)
        frame_ref[k] = frame
        top, bottom = frame[:, :HALO], frame[:, ROWS - HALO :]
        if swap:
            edges[0][k] = jnp.where(lax.axis_index("band") == 0, bottom, top)
        else:
            edges[0][k] = top
            edges[1][k] = bottom


def hot_rows(taps, shift_lane, width, used=None):
    lane = iota((TAPS, width), 1)
    tap = iota((TAPS, width), 0)
    hot = lane == shift_lane(tap)
    if used is not None:
        hot = jnp.logical_and(hot, used(tap))
    hot = hot.astype(F32).astype(BF16)
    return jnp.dot(taps, hot, preferred_element_type=F32)


def table_kernel(bands, up_ref, taps_hbm, spatial_hbm, table_ref, own_ref, halo_ref, taps_ref, spatial_ref, sems):
    copies = start_copies(((taps_hbm, taps_ref), (spatial_hbm, spatial_ref)), sems)
    for copy in copies:
        copy.wait()
    taps = [taps_ref[b].astype(F32) for b in range(BASIS)]
    blank = [jnp.zeros((GROUPS - BASIS, TAPS), F32)]
    column, line_taps = (
        jnp.concatenate([tap[i : i + 1] for tap in taps] + blank, axis=0).astype(BF16) for i in range(2)
    )
    low = LANES // 2 - MARGIN
    lines = hot_rows(column, lambda tap: (-low - tap) % LANES, LANES)
    gap = iota((PAIR, LANES), 0) - iota((PAIR, LANES), 1) - low
    inside = jnp.logical_and(gap >= 0, gap < TAPS)
    for b in range(table_ref.shape[1] // LANES):
        if b < BASIS:
            line = jnp.broadcast_to(lines[b : b + 1], (PAIR, LANES))
            rolled = pltpu.roll(line, 0, 1, stride=1, stride_axis=0)
            part = jnp.where(inside, rolled, 0.0)
        else:
            part = jnp.zeros((PAIR, LANES), F32)
        table_ref[:, b * LANES : (b + 1) * LANES] = part.astype(BF16)

    visits = own_ref.shape[0]
    row = lax.axis_index("band") * ROWS + iota((ROWS, LANES), 0)
    coord = (2.0 * row.astype(F32) + 1.0) / (ROWS * bands) - 1.0
    spatial = jnp.concatenate([spatial_ref[i] for i in range(3 * visits)], axis=0)

    def fill(out_ref, height, offset, used=None):
        fit = LANES // height
        line = 0.0
        which = iota((GROUPS, LANES), 0)
        for j in range(fit):
            part = hot_rows(
                line_taps, lambda tap: (height * j + tap - offset + 2 * LANES) % LANES, LANES, used
            )
            line = line + jnp.where(which % fit == j, part, 0.0)
        t = iota((ROWS, LANES), 1) % height
        tap = t - iota((ROWS, LANES), 0) + offset
        good = jnp.logical_and(tap >= 0, tap < TAPS)
        width = GROUPS * height
        hot = (iota((BASIS, width), 1) // height == iota((BASIS, width), 0)).astype(F32)
        coef = jnp.dot(spatial, hot, precision=lax.Precision.HIGHEST, preferred_element_type=F32)
        for g in range(GROUPS // fit):
            here = jnp.sum(line[g * fit : (g + 1) * fit], axis=0, keepdims=True)
            rolled = pltpu.roll(jnp.broadcast_to(here, (ROWS, LANES)), 0, 1, stride=1, stride_axis=0)
            taps = jnp.where(good, rolled, 0.0)
            lanes = slice(g * LANES, (g + 1) * LANES)
            for k in range(visits):
                c = coef[3 * k : 3 * k + 3, lanes]
                out_ref[k, :ROWS, lanes] = ((c[0:1] + coord * c[1:2]) * taps).astype(BF16)
                out_ref[k, ROWS:, lanes] = (c[2:3] * taps).astype(BF16)

    fill(own_ref, ROWS, MARGIN)
    up = up_ref[0] > 0
    low = jnp.where(up, 0, MARGIN + 1)
    fill(
        halo_ref,
        HALO,
        jnp.where(up, MARGIN - HALO, MARGIN + ROWS),
        lambda tap: jnp.logical_and(tap >= low, tap < low + MARGIN),
    )


def filter_kernel(order, frame_ref, table_ref, mix_ref, *refs):
    (*others, out_ref, windows, filtered) = refs
    weighing = []
    if order:
        count = 1 + NEAR + len(order)
        others, weighing = others[:-count], others[-count:]
    visits, _, height, _ = frame_ref.shape
    half = LANES // 2
    left = iota((height, LANES), 1) < half
    count = ACROSS * height
    for k in range(visits):
        rolled = [pltpu.roll(frame_ref[k, c].astype(F32), half, 1) for c in range(ACROSS)]
        zero = jnp.zeros((height, LANES), F32)
        padded = [zero] + rolled + [zero]
        pieces = [jnp.where(left, padded[c], padded[c + 1]).astype(BF16) for c in range(ACROSS + 1)]
        for c in range(ACROSS):
            rows = slice(k * count + c * height, k * count + (c + 1) * height)
            windows[rows, :LANES] = pieces[c]
            windows[rows, LANES:] = pieces[c + 1]
    done = table_ref.shape[1] // LANES
    filtered[:, done * height :, :] = jnp.zeros((visits, filtered.shape[1] - done * height, COLS), BF16)
    for p in range(done // 2):
        part = jnp.dot(windows[...], table_ref[:, p * PAIR : (p + 1) * PAIR], preferred_element_type=F32).astype(BF16)
        for k in range(visits):
            for c in range(ACROSS):
                for j in range(2):
                    b = 2 * p + j
                    filtered[k, b * height : (b + 1) * height, c * LANES : (c + 1) * LANES] = part[
                        k * count + c * height : k * count + (c + 1) * height, j * LANES : (j + 1) * LANES
                    ]
    col = (2.0 * iota((1, COLS), 1).astype(F32) + 1.0) / COLS - 1.0
    total, sums = 0.0, [0.0] * ACROSS
    for k in range(visits):
        both = jnp.dot(mix_ref[k], filtered[k], preferred_element_type=F32)
        value = sum((part[k] for part in others), both[:ROWS] + col * both[ROWS:])
        if order:
            weight = weight_of(k, order, *weighing)
            total = total + weight
            for c in range(ACROSS):
                part = value[:, c * LANES : (c + 1) * LANES]
                sums[c] = sums[c] + weight[c * ROWS : (c + 1) * ROWS] * part
        else:
            out_ref[k] = value
    if order:
        for c in range(ACROSS):
            out_ref[0, :, c * LANES : (c + 1) * LANES] = sums[c] / total[c * ROWS : (c + 1) * ROWS]


def weight_of(k, order, hot_ref, *refs):
    nears, fars = refs[:NEAR], sorted_refs(order, refs[NEAR:])
    block = CAP * TILE_ROWS
    span = hot_ref.shape[0] * block
    received = []
    for y in range(NEAR):
        received.append(nears[y][part_of(0, span, k, block), :])
        received += [ref[part_of(y, span, k, block), :] for ref in fars]
    return jnp.dot(hot_ref[k], jnp.concatenate(received, axis=0), preferred_element_type=F32)


def shape(dims, kind):
    return jax.ShapeDtypeStruct(dims, kind)


def filter_rows(frame, table, mix, before, name, order=(), weighing=()):
    visits, _, height, _ = frame.shape
    return pl.pallas_call(
        functools.partial(filter_kernel, order),
        out_shape=shape((1 if order else visits, ROWS, COLS), F32),
        in_specs=[vmem()] * (3 + len(before) + len(weighing)),
        out_specs=vmem(),
        scratch_shapes=[
            pltpu.VMEM((visits * ACROSS * height, PAIR), BF16),
            pltpu.VMEM((visits, GROUPS * height, COLS), BF16),
        ],
        compiler_params=params(),
        cost_estimate=cost(4 * visits * ACROSS * height * PAIR * BASIS * LANES, 4 * 1024 * 1024),
        name=name,
    )(frame, table, mix, *before, *weighing)


def regroup(parts, order, count, span, tail, after, name):
    rows = len(parts) * span + (TILE_ROWS if tail else 0)
    return pl.pallas_call(
        functools.partial(regroup_kernel, order, span, len(after)),
        out_shape=(shape((rows, LANES), BF16),) * (count - 1),
        in_specs=[vmem()] * len(parts) + [pl.BlockSpec(memory_space=pl.ANY)] * len(after),
        out_specs=(vmem(),) * (count - 1),
        compiler_params=params(),
        name=name,
    )(*parts, *after)


def per_device(tile_flux, tile_weight, dest_patch, dest_block, basis, spatial):
    visits, tile_count, tile_height, tile_width = tile_flux.shape
    patches, bands = lax.axis_size("patch"), lax.axis_size("band")
    band = lax.axis_index("band")
    far = patches // NEAR
    depth = tile_count * tile_height
    block = CAP * TILE_ROWS
    flux = tile_flux.reshape(visits, depth, tile_width)
    weight = tile_weight.reshape(visits, depth, tile_width)

    def swap(value, step):
        return lax.ppermute(value, "patch", [(i, i ^ step) for i in range(patches)])

    def shift(value, step):
        return lax.ppermute(value, "patch", [(i, (i + step * NEAR) % patches) for i in range(patches)])

    span = visits * block
    fars = range(1, far)
    packed = pl.pallas_call(
        functools.partial(pack_kernel, far),
        out_shape=(shape((NEAR * span + TILE_ROWS, LANES), BF16),) * (far - 1)
        + (shape(((far + 1) * span + TILE_ROWS, LANES), BF16),) * NEAR,
        in_specs=[hbm()] * 4,
        out_specs=(vmem(),) * (far - 1 + NEAR),
        scratch_shapes=[
            pltpu.VMEM(dest_patch.shape, I32),
            pltpu.VMEM(dest_block.shape, I32),
            pltpu.VMEM(flux.shape, BF16),
            pltpu.VMEM(weight.shape, BF16),
            pltpu.SemaphoreType.DMA((4,)),
        ],
        compiler_params=params(),
        name="pack",
    )(*map(in_hbm, (dest_patch, dest_block, flux, weight)))
    first = list(fars)
    chunks = [shift(packed[x - 1], x) for x in first]
    nears = [packed[far - 1]] + [swap(packed[far - 1 + y], y) for y in range(1, NEAR)]

    coefs = spatial.reshape(visits * 3, 1, BASIS)
    taps = basis.transpose(1, 0, 2)

    def tables(up):
        return pl.pallas_call(
            functools.partial(table_kernel, bands),
            out_shape=(
                shape((PAIR, 2 * pl.cdiv(BASIS, 2) * LANES), BF16),
                shape((visits, 2 * ROWS, GROUPS * ROWS), BF16),
                shape((visits, 2 * ROWS, GROUPS * HALO), BF16),
            ),
            in_specs=[smem()] + [hbm()] * 2,
            out_specs=(vmem(),) * 3,
            scratch_shapes=[
                pltpu.VMEM(taps.shape, BF16),
                pltpu.VMEM(coefs.shape, F32),
                pltpu.SemaphoreType.DMA((2,)),
            ],
            compiler_params=params(),
            cost_estimate=cost(10**9, 4 * 1024 * 1024),
            name="tables",
        )(up.reshape(1).astype(I32), in_hbm(taps), in_hbm(coefs))

    if bands == 2:
        ups = [band]
    else:
        ups = [jnp.int32(1), jnp.int32(0)]
    built = [tables(up) for up in ups]
    table, own_mix, _ = built[0]
    flux_sent = regroup(chunks, first, NEAR, span, True, [own_mix], "regroup_flux")
    others = [swap(flux_sent[y - 1], y) for y in range(1, NEAR)]
    weight_sent = regroup(nears, list(range(NEAR)), far, span, False, [flux_sent[0]], "regroup_weight")
    order = sorted(fars, key=lambda x: (x != far // 2, x))
    weights = [shift(weight_sent[x - 1], x) for x in order]

    edge_shape = shape((visits, ACROSS, HALO, LANES), BF16)
    edge_count = 1 if bands == 2 else 2
    frame, hot, *edges = pl.pallas_call(
        functools.partial(place_kernel, far, first, bands == 2),
        out_shape=(
            shape((visits, ACROSS, ROWS, LANES), BF16),
            shape((visits, ACROSS * ROWS, patches * block), BF16),
        )
        + (edge_shape,) * edge_count,
        in_specs=[vmem()] * (far + 2 * NEAR - 2),
        out_specs=(vmem(),) * (2 + edge_count),
        compiler_params=params(),
        name="place_flux",
    )(*chunks, *others, *nears)

    if bands == 2:
        halos = [lax.ppermute(edges[0], "band", [(0, 1), (1, 0)])]
    else:
        down = [(i, i + 1) for i in range(bands - 1)]
        halos = [
            lax.ppermute(edges[1], "band", down),
            lax.ppermute(edges[0], "band", [(j, i) for i, j in down]),
        ]
    value = filter_rows(frame, table, own_mix, [], "filter_own")
    for halo, (_, _, halo_mix) in zip(halos[:-1], built):
        value = filter_rows(halo, table, halo_mix, [value], "filter_halo")
    weighing = (hot, *nears, *weights)
    return filter_rows(halos[-1], table, built[-1][2], [value], "filter_halo_weigh", order, weighing)


def solution(mesh):
    in_specs = (
        P(None, ("patch", "band"), None, None),
        P(None, ("patch", "band"), None, None),
        P(None, ("patch", "band")),
        P(None, ("patch", "band")),
        P(),
        P("patch", None, None, None),
    )
    out_specs = P("patch", "band", None)
    return jax.shard_map(
        per_device, mesh=mesh, in_specs=in_specs, out_specs=out_specs, check_vma=False
    )
```

```python
import functools

import jax
import jax.numpy as jnp
from jax import lax
from jax.experimental import pallas as pl
from jax.experimental.pallas import tpu as pltpu
from jax.sharding import PartitionSpec as P

BASIS = 21
GROUPS = 24
TAPS = 31
MARGIN = TAPS // 2
ROWS = 32
COLS = 512
TILE_ROWS = 8
LANES = 128
ACROSS = COLS // LANES
DOWN = ROWS // TILE_ROWS
CAP = 2
NEAR = 4
HALO = 16
PAIR = 2 * LANES
F32 = jnp.float32
BF16 = jnp.bfloat16
I32 = jnp.int32


def iota(shape, dim):
    return lax.broadcasted_iota(I32, shape, dim)


def vmem():
    return pl.BlockSpec(memory_space=pltpu.VMEM)


def smem():
    return pl.BlockSpec(memory_space=pltpu.SMEM)


def hbm():
    return pl.BlockSpec(memory_space=pltpu.HBM)


def in_hbm(value):
    return pltpu.with_memory_space_constraint(value, pltpu.HBM)


def params():
    return pltpu.CompilerParams(vmem_limit_bytes=40 * 1024 * 1024)


def cost(flops, moved):
    return pl.CostEstimate(flops=flops, bytes_accessed=moved, transcendentals=0)


def slots_of(dest):
    count = dest.shape[1]
    lane = iota(dest.shape, 1)
    ordinal = jnp.zeros(dest.shape, I32)
    for t in range(count - 1):
        same = jnp.logical_and(dest == dest[:, t : t + 1], lane > t)
        ordinal = ordinal + jnp.where(same, 1, 0)
    return dest * CAP + ordinal


def spread(values, width, repeat):
    m = values.shape[1]
    hot = (iota((m, width), 1) // repeat == iota((m, width), 0)).astype(F32).astype(BF16)
    return jnp.dot(values.astype(F32).astype(BF16), hot, preferred_element_type=F32).astype(I32)


def start_copies(pairs, sems):
    copies = [pltpu.make_async_copy(src, dst, sems.at[i]) for i, (src, dst) in enumerate(pairs)]
    for copy in copies:
        copy.start()
    return copies


def sort_visit(goal, tiles, slots):
    row = iota((slots * TILE_ROWS, goal.shape[1]), 0)
    hot = jnp.where(row == goal, 1.0, 0.0).astype(BF16)
    return jnp.dot(hot, tiles, preferred_element_type=F32).astype(BF16)


def pack_kernel(far, dest_hbm, block_hbm, flux_hbm, weight_hbm, *refs):
    far_out, near_out = refs[: far - 1], refs[far - 1 : far - 1 + NEAR]
    landing, sems = refs[far - 1 + NEAR : -1], refs[-1]
    copies = start_copies(zip((dest_hbm, block_hbm, flux_hbm, weight_hbm), landing), sems)
    dest_ref, block_ref, flux_ref, weight_ref = landing
    visits, depth, _ = flux_ref.shape
    block = CAP * TILE_ROWS
    span = visits * block
    copies[0].wait()
    copies[1].wait()
    dest, me = dest_ref[...], lax.axis_index("patch")
    across = (dest // NEAR - me // NEAR + far) % far
    slot = slots_of(across * NEAR + jnp.bitwise_xor(dest % NEAR, me % NEAR))
    goal = spread(slot, depth, TILE_ROWS) * TILE_ROWS + iota((visits, depth), 1) % TILE_ROWS
    place = block_ref[...] % ACROSS * DOWN + block_ref[...] // ACROSS + 1
    lane = iota((TILE_ROWS, LANES), 1)
    for x in range(far):
        note = jnp.zeros((TILE_ROWS, LANES), F32)
        for y in range(NEAR):
            for o in range(CAP):
                chosen = slot == CAP * (x * NEAR + y) + o
                value = jnp.sum(jnp.where(chosen, place, 0).astype(F32), axis=1, keepdims=True)
                value = jnp.concatenate([value, jnp.zeros((TILE_ROWS - visits, 1), F32)], axis=0)
                note = jnp.where(lane == CAP * (y * far + x) + o, value, note)
        note = note.astype(BF16)
        if x:
            far_out[x - 1][NEAR * span :, :] = note
        else:
            for out in near_out:
                out[(far + 1) * span :, :] = note
    copies[2].wait()
    copies[3].wait()
    for k in range(visits):
        both = jnp.concatenate([flux_ref[k], weight_ref[k]], axis=1)
        moved = sort_visit(goal[k : k + 1], both, far * NEAR * CAP)
        for x in range(far):
            for y in range(NEAR):
                rel = x * NEAR + y
                part = moved[rel * block : (rel + 1) * block]
                if x:
                    far_out[x - 1][part_of(y, span, k, block), :] = part[:, :LANES]
                else:
                    near_out[y][part_of(far, span, k, block), :] = part[:, :LANES]
                near_out[y][part_of(x, span, k, block), :] = part[:, LANES:]


def part_of(i, span, k, block):
    return slice(i * span + k * block, i * span + (k + 1) * block)


def sorted_refs(order, refs):
    return [ref for _, ref in sorted(zip(order, refs), key=lambda pair: pair[0])]


def regroup_kernel(order, span, skip, *refs):
    count = len(order)
    ins = sorted_refs(order, refs)
    outs = refs[count + skip :]
    for j, out in enumerate(outs):
        for i, part in enumerate(ins):
            out[i * span : (i + 1) * span, :] = part[(j + 1) * span : (j + 2) * span, :]
        if out.shape[0] > count * span:
            tail = sum(part[part.shape[0] - TILE_ROWS :, :].astype(F32) for part in ins)
            out[count * span :, :] = tail.astype(BF16)


def placing(note, senders):
    width = senders * CAP * TILE_ROWS
    hot = (iota((LANES, width), 1) // TILE_ROWS == iota((LANES, width), 0)).astype(F32).astype(BF16)
    place = jnp.dot(note.astype(BF16), hot, preferred_element_type=F32).astype(I32) - 1
    return place * TILE_ROWS + iota((TILE_ROWS, width), 1) % TILE_ROWS


def arrived(far, order, refs, visits):
    chunks, others = sorted_refs(order, refs[: far - 1]), refs[far - 1 : far + NEAR - 2]
    nears = refs[far + NEAR - 2 : far + 2 * NEAR - 2]
    block = CAP * TILE_ROWS
    span = visits * block
    path = iota((TILE_ROWS, LANES), 1) // (CAP * far)
    note = jnp.zeros((TILE_ROWS, LANES), F32)
    for y in range(NEAR):
        tails = [nears[y]] + (list(chunks) if y == 0 else [others[y - 1]])
        tail = sum(ref[ref.shape[0] - TILE_ROWS :, :].astype(F32) for ref in tails)
        note = jnp.where(path == y, tail, note)

    def rows(k):
        received = []
        for y in range(NEAR):
            received.append(nears[y][part_of(far, span, k, block), :])
            for x in range(1, far):
                if y:
                    received.append(others[y - 1][part_of(x - 1, span, k, block), :])
                else:
                    received.append(chunks[x - 1][part_of(0, span, k, block), :])
        return jnp.concatenate(received, axis=0)

    return placing(note, far * NEAR), rows


def hot_of(row, goal):
    return jnp.where(row == goal, 1.0, 0.0).astype(BF16)


def edge_kernel(far, order, count, *refs):
    edges = refs[far + 2 * NEAR - 2 :]
    goal, rows = arrived(far, order, refs, edges[0].shape[0])
    line = iota((ACROSS * HALO, goal.shape[1]), 0)
    line = line // HALO * ROWS + line % HALO
    low = ROWS - HALO
    starts = [jnp.where(lax.axis_index("band") == 0, low, 0)] if count == 1 else [0, low]
    for k in range(edges[0].shape[0]):
        received = rows(k)
        for edge, start in zip(edges, starts):
            hot = hot_of(line + start, goal[k : k + 1])
            part = jnp.dot(hot, received, preferred_element_type=F32).astype(BF16)
            edge[k] = part.reshape(ACROSS, HALO, LANES)


def place_kernel(far, order, *refs):
    frame_ref, hot_ref = refs[-2:]
    goal, rows = arrived(far, order, refs, frame_ref.shape[0])
    row = iota((ACROSS * ROWS, goal.shape[1]), 0)
    for k in range(frame_ref.shape[0]):
        hot = hot_of(row, goal[k : k + 1])
        hot_ref[k] = hot
        frame = jnp.dot(hot, rows(k), preferred_element_type=F32).astype(BF16)
        frame_ref[k] = frame.reshape(ACROSS, ROWS, LANES)


def hot_rows(taps, shift_lane, width, used=None):
    lane = iota((TAPS, width), 1)
    tap = iota((TAPS, width), 0)
    hot = lane == shift_lane(tap)
    if used is not None:
        hot = jnp.logical_and(hot, used(tap))
    hot = hot.astype(F32).astype(BF16)
    return jnp.dot(taps, hot, preferred_element_type=F32)


def table_kernel(bands, up_ref, taps_hbm, spatial_hbm, table_ref, own_ref, halo_ref, taps_ref, spatial_ref, sems):
    copies = start_copies(((taps_hbm, taps_ref), (spatial_hbm, spatial_ref)), sems)
    for copy in copies:
        copy.wait()
    taps = [taps_ref[b].astype(F32) for b in range(BASIS)]
    blank = [jnp.zeros((GROUPS - BASIS, TAPS), F32)]
    column, line_taps = (
        jnp.concatenate([tap[i : i + 1] for tap in taps] + blank, axis=0).astype(BF16) for i in range(2)
    )
    low = LANES // 2 - MARGIN
    lines = hot_rows(column, lambda tap: (-low - tap) % LANES, LANES)
    gap = iota((PAIR, LANES), 0) - iota((PAIR, LANES), 1) - low
    inside = jnp.logical_and(gap >= 0, gap < TAPS)
    for b in range(table_ref.shape[1] // LANES):
        if b < BASIS:
            line = jnp.broadcast_to(lines[b : b + 1], (PAIR, LANES))
            rolled = pltpu.roll(line, 0, 1, stride=1, stride_axis=0)
            part = jnp.where(inside, rolled, 0.0)
        else:
            part = jnp.zeros((PAIR, LANES), F32)
        table_ref[:, b * LANES : (b + 1) * LANES] = part.astype(BF16)

    visits = own_ref.shape[0]
    row = lax.axis_index("band") * ROWS + iota((ROWS, LANES), 0)
    coord = (2.0 * row.astype(F32) + 1.0) / (ROWS * bands) - 1.0
    spatial = jnp.concatenate([spatial_ref[i] for i in range(3 * visits)], axis=0)

    def fill(out_ref, height, offset, used=None):
        fit = LANES // height
        line = 0.0
        which = iota((GROUPS, LANES), 0)
        for j in range(fit):
            part = hot_rows(
                line_taps, lambda tap: (height * j + tap - offset + 2 * LANES) % LANES, LANES, used
            )
            line = line + jnp.where(which % fit == j, part, 0.0)
        t = iota((ROWS, LANES), 1) % height
        tap = t - iota((ROWS, LANES), 0) + offset
        good = jnp.logical_and(tap >= 0, tap < TAPS)
        width = GROUPS * height
        hot = (iota((BASIS, width), 1) // height == iota((BASIS, width), 0)).astype(F32)
        coef = jnp.dot(spatial, hot, precision=lax.Precision.HIGHEST, preferred_element_type=F32)
        for g in range(GROUPS // fit):
            here = jnp.sum(line[g * fit : (g + 1) * fit], axis=0, keepdims=True)
            rolled = pltpu.roll(jnp.broadcast_to(here, (ROWS, LANES)), 0, 1, stride=1, stride_axis=0)
            taps = jnp.where(good, rolled, 0.0)
            lanes = slice(g * LANES, (g + 1) * LANES)
            for k in range(visits):
                c = coef[3 * k : 3 * k + 3, lanes]
                out_ref[k, :ROWS, lanes] = ((c[0:1] + coord * c[1:2]) * taps).astype(BF16)
                out_ref[k, ROWS:, lanes] = (c[2:3] * taps).astype(BF16)

    fill(own_ref, ROWS, MARGIN)
    up = up_ref[0] > 0
    low = jnp.where(up, 0, MARGIN + 1)
    fill(
        halo_ref,
        HALO,
        jnp.where(up, MARGIN - HALO, MARGIN + ROWS),
        lambda tap: jnp.logical_and(tap >= low, tap < low + MARGIN),
    )


def filter_kernel(order, frame_ref, table_ref, mix_ref, *refs):
    (*others, out_ref, windows, filtered) = refs
    weighing = []
    if order:
        count = 1 + NEAR + len(order)
        others, weighing = others[:-count], others[-count:]
    visits, _, height, _ = frame_ref.shape
    half = LANES // 2
    left = iota((height, LANES), 1) < half
    count = ACROSS * height
    for k in range(visits):
        rolled = [pltpu.roll(frame_ref[k, c].astype(F32), half, 1) for c in range(ACROSS)]
        zero = jnp.zeros((height, LANES), F32)
        padded = [zero] + rolled + [zero]
        pieces = [jnp.where(left, padded[c], padded[c + 1]).astype(BF16) for c in range(ACROSS + 1)]
        for c in range(ACROSS):
            rows = slice(k * count + c * height, k * count + (c + 1) * height)
            windows[rows, :LANES] = pieces[c]
            windows[rows, LANES:] = pieces[c + 1]
    done = table_ref.shape[1] // LANES
    filtered[:, done * height :, :] = jnp.zeros((visits, filtered.shape[1] - done * height, COLS), BF16)
    for p in range(done // 2):
        part = jnp.dot(windows[...], table_ref[:, p * PAIR : (p + 1) * PAIR], preferred_element_type=F32).astype(BF16)
        for k in range(visits):
            for c in range(ACROSS):
                for j in range(2):
                    b = 2 * p + j
                    filtered[k, b * height : (b + 1) * height, c * LANES : (c + 1) * LANES] = part[
                        k * count + c * height : k * count + (c + 1) * height, j * LANES : (j + 1) * LANES
                    ]
    col = (2.0 * iota((1, COLS), 1).astype(F32) + 1.0) / COLS - 1.0
    total, sums = 0.0, [0.0] * ACROSS
    for k in range(visits):
        both = jnp.dot(mix_ref[k], filtered[k], preferred_element_type=F32)
        value = sum((part[k] for part in others), both[:ROWS] + col * both[ROWS:])
        if order:
            weight = weight_of(k, order, *weighing)
            total = total + weight
            for c in range(ACROSS):
                part = value[:, c * LANES : (c + 1) * LANES]
                sums[c] = sums[c] + weight[c * ROWS : (c + 1) * ROWS] * part
        else:
            out_ref[k] = value
    if order:
        for c in range(ACROSS):
            out_ref[0, :, c * LANES : (c + 1) * LANES] = sums[c] / total[c * ROWS : (c + 1) * ROWS]


def weight_of(k, order, hot_ref, *refs):
    nears, fars = refs[:NEAR], sorted_refs(order, refs[NEAR:])
    block = CAP * TILE_ROWS
    span = hot_ref.shape[0] * block
    received = []
    for y in range(NEAR):
        received.append(nears[y][part_of(0, span, k, block), :])
        received += [ref[part_of(y, span, k, block), :] for ref in fars]
    return jnp.dot(hot_ref[k], jnp.concatenate(received, axis=0), preferred_element_type=F32)


def shape(dims, kind):
    return jax.ShapeDtypeStruct(dims, kind)


def filter_rows(frame, table, mix, before, name, order=(), weighing=()):
    visits, _, height, _ = frame.shape
    return pl.pallas_call(
        functools.partial(filter_kernel, order),
        out_shape=shape((1 if order else visits, ROWS, COLS), F32),
        in_specs=[vmem()] * (3 + len(before) + len(weighing)),
        out_specs=vmem(),
        scratch_shapes=[
            pltpu.VMEM((visits * ACROSS * height, PAIR), BF16),
            pltpu.VMEM((visits, GROUPS * height, COLS), BF16),
        ],
        compiler_params=params(),
        cost_estimate=cost(4 * visits * ACROSS * height * PAIR * BASIS * LANES, 4 * 1024 * 1024),
        name=name,
    )(frame, table, mix, *before, *weighing)


def regroup(parts, order, count, span, tail, after, name):
    rows = len(parts) * span + (TILE_ROWS if tail else 0)
    return pl.pallas_call(
        functools.partial(regroup_kernel, order, span, len(after)),
        out_shape=(shape((rows, LANES), BF16),) * (count - 1),
        in_specs=[vmem()] * len(parts) + [pl.BlockSpec(memory_space=pl.ANY)] * len(after),
        out_specs=(vmem(),) * (count - 1),
        compiler_params=params(),
        name=name,
    )(*parts, *after)


def per_device(tile_flux, tile_weight, dest_patch, dest_block, basis, spatial):
    visits, tile_count, tile_height, tile_width = tile_flux.shape
    patches, bands = lax.axis_size("patch"), lax.axis_size("band")
    band = lax.axis_index("band")
    far = patches // NEAR
    depth = tile_count * tile_height
    block = CAP * TILE_ROWS
    flux = tile_flux.reshape(visits, depth, tile_width)
    weight = tile_weight.reshape(visits, depth, tile_width)

    def swap(value, step):
        return lax.ppermute(value, "patch", [(i, i ^ step) for i in range(patches)])

    def shift(value, step):
        return lax.ppermute(value, "patch", [(i, (i + step * NEAR) % patches) for i in range(patches)])

    span = visits * block
    fars = range(1, far)
    packed = pl.pallas_call(
        functools.partial(pack_kernel, far),
        out_shape=(shape((NEAR * span + TILE_ROWS, LANES), BF16),) * (far - 1)
        + (shape(((far + 1) * span + TILE_ROWS, LANES), BF16),) * NEAR,
        in_specs=[hbm()] * 4,
        out_specs=(vmem(),) * (far - 1 + NEAR),
        scratch_shapes=[
            pltpu.VMEM(dest_patch.shape, I32),
            pltpu.VMEM(dest_block.shape, I32),
            pltpu.VMEM(flux.shape, BF16),
            pltpu.VMEM(weight.shape, BF16),
            pltpu.SemaphoreType.DMA((4,)),
        ],
        compiler_params=params(),
        name="pack",
    )(*map(in_hbm, (dest_patch, dest_block, flux, weight)))
    first = list(fars)
    chunks = [shift(packed[x - 1], x) for x in first]
    nears = [packed[far - 1]] + [swap(packed[far - 1 + y], y) for y in range(1, NEAR)]

    coefs = spatial.reshape(visits * 3, 1, BASIS)
    taps = basis.transpose(1, 0, 2)

    def tables(up):
        return pl.pallas_call(
            functools.partial(table_kernel, bands),
            out_shape=(
                shape((PAIR, 2 * pl.cdiv(BASIS, 2) * LANES), BF16),
                shape((visits, 2 * ROWS, GROUPS * ROWS), BF16),
                shape((visits, 2 * ROWS, GROUPS * HALO), BF16),
            ),
            in_specs=[smem()] + [hbm()] * 2,
            out_specs=(vmem(),) * 3,
            scratch_shapes=[
                pltpu.VMEM(taps.shape, BF16),
                pltpu.VMEM(coefs.shape, F32),
                pltpu.SemaphoreType.DMA((2,)),
            ],
            compiler_params=params(),
            cost_estimate=cost(10**9, 4 * 1024 * 1024),
            name="tables",
        )(up.reshape(1).astype(I32), in_hbm(taps), in_hbm(coefs))

    if bands == 2:
        ups = [band]
    else:
        ups = [jnp.int32(1), jnp.int32(0)]
    built = [tables(up) for up in ups]
    table, own_mix, _ = built[0]
    flux_sent = regroup(chunks, first, NEAR, span, True, [own_mix], "regroup_flux")
    others = [swap(flux_sent[y - 1], y) for y in range(1, NEAR)]
    weight_sent = regroup(nears, list(range(NEAR)), far, span, False, [], "regroup_weight")
    order = sorted(fars, key=lambda x: (x != far // 2, x))
    weights = [shift(weight_sent[x - 1], x) for x in order]

    edge_shape = shape((visits, ACROSS, HALO, LANES), BF16)
    edge_count = 1 if bands == 2 else 2
    received = (*chunks, *others, *nears)
    edges = pl.pallas_call(
        functools.partial(edge_kernel, far, first, edge_count),
        out_shape=(edge_shape,) * edge_count,
        in_specs=[vmem()] * len(received),
        out_specs=(vmem(),) * edge_count,
        compiler_params=params(),
        name="edges",
    )(*received)
    frame, hot = pl.pallas_call(
        functools.partial(place_kernel, far, first),
        out_shape=(
            shape((visits, ACROSS, ROWS, LANES), BF16),
            shape((visits, ACROSS * ROWS, patches * block), BF16),
        ),
        in_specs=[vmem()] * len(received) + [pl.BlockSpec(memory_space=pl.ANY)],
        out_specs=(vmem(),) * 2,
        compiler_params=params(),
        name="place_flux",
    )(*received, edges[0])

    if bands == 2:
        halos = [lax.ppermute(edges[0], "band", [(0, 1), (1, 0)])]
    else:
        down = [(i, i + 1) for i in range(bands - 1)]
        halos = [
            lax.ppermute(edges[1], "band", down),
            lax.ppermute(edges[0], "band", [(j, i) for i, j in down]),
        ]
    value = filter_rows(frame, table, own_mix, [], "filter_own")
    for halo, (_, _, halo_mix) in zip(halos[:-1], built):
        value = filter_rows(halo, table, halo_mix, [value], "filter_halo")
    weighing = (hot, *nears, *weights)
    return filter_rows(halos[-1], table, built[-1][2], [value], "filter_halo_weigh", order, weighing)


def solution(mesh):
    in_specs = (
        P(None, ("patch", "band"), None, None),
        P(None, ("patch", "band"), None, None),
        P(None, ("patch", "band")),
        P(None, ("patch", "band")),
        P(),
        P("patch", None, None, None),
    )
    out_specs = P("patch", "band", None)
    return jax.shard_map(
        per_device, mesh=mesh, in_specs=in_specs, out_specs=out_specs, check_vma=False
    )
```

```python
import functools

import jax
import jax.numpy as jnp
from jax import lax
from jax.experimental import pallas as pl
from jax.experimental.pallas import tpu as pltpu
from jax.sharding import PartitionSpec as P

BASIS = 21
GROUPS = 24
TAPS = 31
MARGIN = TAPS // 2
ROWS = 32
COLS = 512
TILE_ROWS = 8
LANES = 128
ACROSS = COLS // LANES
DOWN = ROWS // TILE_ROWS
CAP = 2
NEAR = 4
HALO = 16
PAIR = 2 * LANES
F32 = jnp.float32
BF16 = jnp.bfloat16
I32 = jnp.int32


def iota(shape, dim):
    return lax.broadcasted_iota(I32, shape, dim)


def vmem():
    return pl.BlockSpec(memory_space=pltpu.VMEM)


def smem():
    return pl.BlockSpec(memory_space=pltpu.SMEM)


def hbm():
    return pl.BlockSpec(memory_space=pltpu.HBM)


def in_hbm(value):
    return pltpu.with_memory_space_constraint(value, pltpu.HBM)


def params():
    return pltpu.CompilerParams(vmem_limit_bytes=40 * 1024 * 1024)


def cost(flops, moved):
    return pl.CostEstimate(flops=flops, bytes_accessed=moved, transcendentals=0)


def slots_of(dest):
    count = dest.shape[1]
    lane = iota(dest.shape, 1)
    ordinal = jnp.zeros(dest.shape, I32)
    for t in range(count - 1):
        same = jnp.logical_and(dest == dest[:, t : t + 1], lane > t)
        ordinal = ordinal + jnp.where(same, 1, 0)
    return dest * CAP + ordinal


def spread(values, width, repeat):
    m = values.shape[1]
    hot = (iota((m, width), 1) // repeat == iota((m, width), 0)).astype(F32).astype(BF16)
    return jnp.dot(values.astype(F32).astype(BF16), hot, preferred_element_type=F32).astype(I32)


def start_copies(pairs, sems):
    copies = [pltpu.make_async_copy(src, dst, sems.at[i]) for i, (src, dst) in enumerate(pairs)]
    for copy in copies:
        copy.start()
    return copies


def sort_visit(goal, tiles, slots):
    row = iota((slots * TILE_ROWS, goal.shape[1]), 0)
    hot = jnp.where(row == goal, 1.0, 0.0).astype(BF16)
    return jnp.dot(hot, tiles, preferred_element_type=F32).astype(BF16)


def pack_kernel(far, dest_hbm, block_hbm, flux_hbm, weight_hbm, *refs):
    far_out, near_out = refs[: far - 1], refs[far - 1 : far - 1 + NEAR]
    landing, sems = refs[far - 1 + NEAR : -1], refs[-1]
    dest_ref, block_ref, flux_ref, weight_ref = landing
    pairs = (dest_hbm, dest_ref), (flux_hbm, flux_ref), (weight_hbm, weight_ref), (block_hbm, block_ref)
    copies = start_copies(pairs, sems)
    visits, depth, _ = flux_ref.shape
    block = CAP * TILE_ROWS
    span = visits * block
    copies[0].wait()
    dest, me = dest_ref[...], lax.axis_index("patch")
    across = (dest // NEAR - me // NEAR + far) % far
    slot = slots_of(across * NEAR + jnp.bitwise_xor(dest % NEAR, me % NEAR))
    goal = spread(slot, depth, TILE_ROWS) * TILE_ROWS + iota((visits, depth), 1) % TILE_ROWS
    for copy in copies[1:]:
        copy.wait()
    for k in range(visits):
        both = jnp.concatenate([flux_ref[k], weight_ref[k]], axis=1)
        moved = sort_visit(goal[k : k + 1], both, far * NEAR * CAP)
        for x in range(far):
            for y in range(NEAR):
                rel = x * NEAR + y
                part = moved[rel * block : (rel + 1) * block]
                if x:
                    far_out[x - 1][part_of(y, span, k, block), :] = part[:, :LANES]
                else:
                    near_out[y][part_of(far, span, k, block), :] = part[:, :LANES]
                near_out[y][part_of(x, span, k, block), :] = part[:, LANES:]
    place = block_ref[...] % ACROSS * DOWN + block_ref[...] // ACROSS + 1
    lane = iota((TILE_ROWS, LANES), 1)
    for x in range(far):
        note = jnp.zeros((TILE_ROWS, LANES), F32)
        for y in range(NEAR):
            for o in range(CAP):
                chosen = slot == CAP * (x * NEAR + y) + o
                value = jnp.sum(jnp.where(chosen, place, 0).astype(F32), axis=1, keepdims=True)
                value = jnp.concatenate([value, jnp.zeros((TILE_ROWS - visits, 1), F32)], axis=0)
                note = jnp.where(lane == CAP * (y * far + x) + o, value, note)
        note = note.astype(BF16)
        if x:
            far_out[x - 1][NEAR * span :, :] = note
        else:
            for out in near_out:
                out[(far + 1) * span :, :] = note


def part_of(i, span, k, block):
    return slice(i * span + k * block, i * span + (k + 1) * block)


def sorted_refs(order, refs):
    return [ref for _, ref in sorted(zip(order, refs), key=lambda pair: pair[0])]


def regroup_kernel(order, span, skip, *refs):
    count = len(order)
    ins = sorted_refs(order, refs)
    outs = refs[count + skip :]
    for j, out in enumerate(outs):
        for i, part in enumerate(ins):
            out[i * span : (i + 1) * span, :] = part[(j + 1) * span : (j + 2) * span, :]
        if out.shape[0] > count * span:
            tail = sum(part[part.shape[0] - TILE_ROWS :, :].astype(F32) for part in ins)
            out[count * span :, :] = tail.astype(BF16)


def placing(note, senders):
    width = senders * CAP * TILE_ROWS
    hot = (iota((LANES, width), 1) // TILE_ROWS == iota((LANES, width), 0)).astype(F32).astype(BF16)
    place = jnp.dot(note.astype(BF16), hot, preferred_element_type=F32).astype(I32) - 1
    return place * TILE_ROWS + iota((TILE_ROWS, width), 1) % TILE_ROWS


def arrived(far, order, refs, visits):
    chunks, others = sorted_refs(order, refs[: far - 1]), refs[far - 1 : far + NEAR - 2]
    nears = refs[far + NEAR - 2 : far + 2 * NEAR - 2]
    block = CAP * TILE_ROWS
    span = visits * block
    path = iota((TILE_ROWS, LANES), 1) // (CAP * far)
    note = jnp.zeros((TILE_ROWS, LANES), F32)
    for y in range(NEAR):
        tails = [nears[y]] + (list(chunks) if y == 0 else [others[y - 1]])
        tail = sum(ref[ref.shape[0] - TILE_ROWS :, :].astype(F32) for ref in tails)
        note = jnp.where(path == y, tail, note)

    def rows(k):
        received = []
        for y in range(NEAR):
            received.append(nears[y][part_of(far, span, k, block), :])
            for x in range(1, far):
                if y:
                    received.append(others[y - 1][part_of(x - 1, span, k, block), :])
                else:
                    received.append(chunks[x - 1][part_of(0, span, k, block), :])
        return jnp.concatenate(received, axis=0)

    return placing(note, far * NEAR), rows


def hot_of(row, goal):
    return jnp.where(row == goal, 1.0, 0.0).astype(BF16)


def edge_kernel(far, order, count, *refs):
    edges = refs[far + 2 * NEAR - 2 :]
    goal, rows = arrived(far, order, refs, edges[0].shape[0])
    line = iota((ACROSS * HALO, goal.shape[1]), 0)
    line = line // HALO * ROWS + line % HALO
    low = ROWS - HALO
    starts = [jnp.where(lax.axis_index("band") == 0, low, 0)] if count == 1 else [0, low]
    for k in range(edges[0].shape[0]):
        received = rows(k)
        for edge, start in zip(edges, starts):
            hot = hot_of(line + start, goal[k : k + 1])
            part = jnp.dot(hot, received, preferred_element_type=F32).astype(BF16)
            edge[k] = part.reshape(ACROSS, HALO, LANES)


def place_kernel(far, order, *refs):
    frame_ref, hot_ref = refs[-2:]
    goal, rows = arrived(far, order, refs, frame_ref.shape[0])
    row = iota((ACROSS * ROWS, goal.shape[1]), 0)
    for k in range(frame_ref.shape[0]):
        hot = hot_of(row, goal[k : k + 1])
        hot_ref[k] = hot
        frame = jnp.dot(hot, rows(k), preferred_element_type=F32).astype(BF16)
        frame_ref[k] = frame.reshape(ACROSS, ROWS, LANES)


def hot_rows(taps, shift_lane, width, used=None):
    lane = iota((TAPS, width), 1)
    tap = iota((TAPS, width), 0)
    hot = lane == shift_lane(tap)
    if used is not None:
        hot = jnp.logical_and(hot, used(tap))
    hot = hot.astype(F32).astype(BF16)
    return jnp.dot(taps, hot, preferred_element_type=F32)


def table_kernel(bands, up_ref, taps_hbm, spatial_hbm, table_ref, own_ref, halo_ref, taps_ref, spatial_ref, sems):
    copies = start_copies(((taps_hbm, taps_ref), (spatial_hbm, spatial_ref)), sems)
    for copy in copies:
        copy.wait()
    taps = [taps_ref[b].astype(F32) for b in range(BASIS)]
    blank = [jnp.zeros((GROUPS - BASIS, TAPS), F32)]
    column, line_taps = (
        jnp.concatenate([tap[i : i + 1] for tap in taps] + blank, axis=0).astype(BF16) for i in range(2)
    )
    low = LANES // 2 - MARGIN
    lines = hot_rows(column, lambda tap: (-low - tap) % LANES, LANES)
    gap = iota((PAIR, LANES), 0) - iota((PAIR, LANES), 1) - low
    inside = jnp.logical_and(gap >= 0, gap < TAPS)
    for b in range(table_ref.shape[1] // LANES):
        if b < BASIS:
            line = jnp.broadcast_to(lines[b : b + 1], (PAIR, LANES))
            rolled = pltpu.roll(line, 0, 1, stride=1, stride_axis=0)
            part = jnp.where(inside, rolled, 0.0)
        else:
            part = jnp.zeros((PAIR, LANES), F32)
        table_ref[:, b * LANES : (b + 1) * LANES] = part.astype(BF16)

    visits = own_ref.shape[0]
    row = lax.axis_index("band") * ROWS + iota((ROWS, LANES), 0)
    coord = (2.0 * row.astype(F32) + 1.0) / (ROWS * bands) - 1.0
    spatial = jnp.concatenate([spatial_ref[i] for i in range(3 * visits)], axis=0)

    def fill(out_ref, height, offset, used=None):
        fit = LANES // height
        line = 0.0
        which = iota((GROUPS, LANES), 0)
        for j in range(fit):
            part = hot_rows(
                line_taps, lambda tap: (height * j + tap - offset + 2 * LANES) % LANES, LANES, used
            )
            line = line + jnp.where(which % fit == j, part, 0.0)
        t = iota((ROWS, LANES), 1) % height
        tap = t - iota((ROWS, LANES), 0) + offset
        good = jnp.logical_and(tap >= 0, tap < TAPS)
        width = GROUPS * height
        hot = (iota((BASIS, width), 1) // height == iota((BASIS, width), 0)).astype(F32)
        coef = jnp.dot(spatial, hot, precision=lax.Precision.HIGHEST, preferred_element_type=F32)
        for g in range(GROUPS // fit):
            here = jnp.sum(line[g * fit : (g + 1) * fit], axis=0, keepdims=True)
            rolled = pltpu.roll(jnp.broadcast_to(here, (ROWS, LANES)), 0, 1, stride=1, stride_axis=0)
            taps = jnp.where(good, rolled, 0.0)
            lanes = slice(g * LANES, (g + 1) * LANES)
            for k in range(visits):
                c = coef[3 * k : 3 * k + 3, lanes]
                out_ref[k, :ROWS, lanes] = ((c[0:1] + coord * c[1:2]) * taps).astype(BF16)
                out_ref[k, ROWS:, lanes] = (c[2:3] * taps).astype(BF16)

    fill(own_ref, ROWS, MARGIN)
    up = up_ref[0] > 0
    low = jnp.where(up, 0, MARGIN + 1)
    fill(
        halo_ref,
        HALO,
        jnp.where(up, MARGIN - HALO, MARGIN + ROWS),
        lambda tap: jnp.logical_and(tap >= low, tap < low + MARGIN),
    )


def filter_kernel(order, frame_ref, table_ref, mix_ref, *refs):
    (*others, out_ref, windows, filtered) = refs
    weighing = []
    if order:
        count = 1 + NEAR + len(order)
        others, weighing = others[:-count], others[-count:]
    visits, _, height, _ = frame_ref.shape
    half = LANES // 2
    left = iota((height, LANES), 1) < half
    count = ACROSS * height
    for k in range(visits):
        rolled = [pltpu.roll(frame_ref[k, c].astype(F32), half, 1) for c in range(ACROSS)]
        zero = jnp.zeros((height, LANES), F32)
        padded = [zero] + rolled + [zero]
        pieces = [jnp.where(left, padded[c], padded[c + 1]).astype(BF16) for c in range(ACROSS + 1)]
        for c in range(ACROSS):
            rows = slice(k * count + c * height, k * count + (c + 1) * height)
            windows[rows, :LANES] = pieces[c]
            windows[rows, LANES:] = pieces[c + 1]
    done = table_ref.shape[1] // LANES
    filtered[:, done * height :, :] = jnp.zeros((visits, filtered.shape[1] - done * height, COLS), BF16)
    for p in range(done // 2):
        part = jnp.dot(windows[...], table_ref[:, p * PAIR : (p + 1) * PAIR], preferred_element_type=F32).astype(BF16)
        for k in range(visits):
            for c in range(ACROSS):
                for j in range(2):
                    b = 2 * p + j
                    filtered[k, b * height : (b + 1) * height, c * LANES : (c + 1) * LANES] = part[
                        k * count + c * height : k * count + (c + 1) * height, j * LANES : (j + 1) * LANES
                    ]
    col = (2.0 * iota((1, COLS), 1).astype(F32) + 1.0) / COLS - 1.0
    total, sums = 0.0, [0.0] * ACROSS
    for k in range(visits):
        both = jnp.dot(mix_ref[k], filtered[k], preferred_element_type=F32)
        value = sum((part[k] for part in others), both[:ROWS] + col * both[ROWS:])
        if order:
            weight = weight_of(k, order, *weighing)
            total = total + weight
            for c in range(ACROSS):
                part = value[:, c * LANES : (c + 1) * LANES]
                sums[c] = sums[c] + weight[c * ROWS : (c + 1) * ROWS] * part
        else:
            out_ref[k] = value
    if order:
        for c in range(ACROSS):
            out_ref[0, :, c * LANES : (c + 1) * LANES] = sums[c] / total[c * ROWS : (c + 1) * ROWS]


def weight_of(k, order, hot_ref, *refs):
    nears, fars = refs[:NEAR], sorted_refs(order, refs[NEAR:])
    block = CAP * TILE_ROWS
    span = hot_ref.shape[0] * block
    received = []
    for y in range(NEAR):
        received.append(nears[y][part_of(0, span, k, block), :])
        received += [ref[part_of(y, span, k, block), :] for ref in fars]
    return jnp.dot(hot_ref[k], jnp.concatenate(received, axis=0), preferred_element_type=F32)


def shape(dims, kind):
    return jax.ShapeDtypeStruct(dims, kind)


def filter_rows(frame, table, mix, before, name, order=(), weighing=()):
    visits, _, height, _ = frame.shape
    return pl.pallas_call(
        functools.partial(filter_kernel, order),
        out_shape=shape((1 if order else visits, ROWS, COLS), F32),
        in_specs=[vmem()] * (3 + len(before) + len(weighing)),
        out_specs=vmem(),
        scratch_shapes=[
            pltpu.VMEM((visits * ACROSS * height, PAIR), BF16),
            pltpu.VMEM((visits, GROUPS * height, COLS), BF16),
        ],
        compiler_params=params(),
        cost_estimate=cost(4 * visits * ACROSS * height * PAIR * BASIS * LANES, 4 * 1024 * 1024),
        name=name,
    )(frame, table, mix, *before, *weighing)


def regroup(parts, order, count, span, tail, after, name):
    rows = len(parts) * span + (TILE_ROWS if tail else 0)
    return pl.pallas_call(
        functools.partial(regroup_kernel, order, span, len(after)),
        out_shape=(shape((rows, LANES), BF16),) * (count - 1),
        in_specs=[vmem()] * len(parts) + [pl.BlockSpec(memory_space=pl.ANY)] * len(after),
        out_specs=(vmem(),) * (count - 1),
        compiler_params=params(),
        name=name,
    )(*parts, *after)


def per_device(tile_flux, tile_weight, dest_patch, dest_block, basis, spatial):
    visits, tile_count, tile_height, tile_width = tile_flux.shape
    patches, bands = lax.axis_size("patch"), lax.axis_size("band")
    band = lax.axis_index("band")
    far = patches // NEAR
    depth = tile_count * tile_height
    block = CAP * TILE_ROWS
    flux = tile_flux.reshape(visits, depth, tile_width)
    weight = tile_weight.reshape(visits, depth, tile_width)

    def swap(value, step):
        return lax.ppermute(value, "patch", [(i, i ^ step) for i in range(patches)])

    def shift(value, step):
        return lax.ppermute(value, "patch", [(i, (i + step * NEAR) % patches) for i in range(patches)])

    span = visits * block
    fars = range(1, far)
    packed = pl.pallas_call(
        functools.partial(pack_kernel, far),
        out_shape=(shape((NEAR * span + TILE_ROWS, LANES), BF16),) * (far - 1)
        + (shape(((far + 1) * span + TILE_ROWS, LANES), BF16),) * NEAR,
        in_specs=[hbm()] * 4,
        out_specs=(vmem(),) * (far - 1 + NEAR),
        scratch_shapes=[
            pltpu.VMEM(dest_patch.shape, I32),
            pltpu.VMEM(dest_block.shape, I32),
            pltpu.VMEM(flux.shape, BF16),
            pltpu.VMEM(weight.shape, BF16),
            pltpu.SemaphoreType.DMA((4,)),
        ],
        compiler_params=params(),
        name="pack",
    )(*map(in_hbm, (dest_patch, dest_block, flux, weight)))
    first = list(fars)
    chunks = [shift(packed[x - 1], x) for x in first]
    nears = [packed[far - 1]] + [swap(packed[far - 1 + y], y) for y in range(1, NEAR)]

    coefs = spatial.reshape(visits * 3, 1, BASIS)
    taps = basis.transpose(1, 0, 2)

    def tables(up):
        return pl.pallas_call(
            functools.partial(table_kernel, bands),
            out_shape=(
                shape((PAIR, 2 * pl.cdiv(BASIS, 2) * LANES), BF16),
                shape((visits, 2 * ROWS, GROUPS * ROWS), BF16),
                shape((visits, 2 * ROWS, GROUPS * HALO), BF16),
            ),
            in_specs=[smem()] + [hbm()] * 2,
            out_specs=(vmem(),) * 3,
            scratch_shapes=[
                pltpu.VMEM(taps.shape, BF16),
                pltpu.VMEM(coefs.shape, F32),
                pltpu.SemaphoreType.DMA((2,)),
            ],
            compiler_params=params(),
            cost_estimate=cost(10**9, 4 * 1024 * 1024),
            name="tables",
        )(up.reshape(1).astype(I32), in_hbm(taps), in_hbm(coefs))

    if bands == 2:
        ups = [band]
    else:
        ups = [jnp.int32(1), jnp.int32(0)]
    built = [tables(up) for up in ups]
    table, own_mix, _ = built[0]
    flux_sent = regroup(chunks, first, NEAR, span, True, [own_mix], "regroup_flux")
    others = [swap(flux_sent[y - 1], y) for y in range(1, NEAR)]
    weight_sent = regroup(nears, list(range(NEAR)), far, span, False, [], "regroup_weight")
    order = sorted(fars, key=lambda x: (x != far // 2, x))
    weights = [shift(weight_sent[x - 1], x) for x in order]

    edge_shape = shape((visits, ACROSS, HALO, LANES), BF16)
    edge_count = 1 if bands == 2 else 2
    received = (*chunks, *others, *nears)
    edges = pl.pallas_call(
        functools.partial(edge_kernel, far, first, edge_count),
        out_shape=(edge_shape,) * edge_count,
        in_specs=[vmem()] * len(received),
        out_specs=(vmem(),) * edge_count,
        compiler_params=params(),
        name="edges",
    )(*received)
    frame, hot = pl.pallas_call(
        functools.partial(place_kernel, far, first),
        out_shape=(
            shape((visits, ACROSS, ROWS, LANES), BF16),
            shape((visits, ACROSS * ROWS, patches * block), BF16),
        ),
        in_specs=[vmem()] * len(received) + [pl.BlockSpec(memory_space=pl.ANY)],
        out_specs=(vmem(),) * 2,
        compiler_params=params(),
        name="place_flux",
    )(*received, edges[0])

    if bands == 2:
        halos = [lax.ppermute(edges[0], "band", [(0, 1), (1, 0)])]
    else:
        down = [(i, i + 1) for i in range(bands - 1)]
        halos = [
            lax.ppermute(edges[1], "band", down),
            lax.ppermute(edges[0], "band", [(j, i) for i, j in down]),
        ]
    value = filter_rows(frame, table, own_mix, [], "filter_own")
    for halo, (_, _, halo_mix) in zip(halos[:-1], built):
        value = filter_rows(halo, table, halo_mix, [value], "filter_halo")
    weighing = (hot, *nears, *weights)
    return filter_rows(halos[-1], table, built[-1][2], [value], "filter_halo_weigh", order, weighing)


def solution(mesh):
    in_specs = (
        P(None, ("patch", "band"), None, None),
        P(None, ("patch", "band"), None, None),
        P(None, ("patch", "band")),
        P(None, ("patch", "band")),
        P(),
        P("patch", None, None, None),
    )
    out_specs = P("patch", "band", None)
    return jax.shard_map(
        per_device, mesh=mesh, in_specs=in_specs, out_specs=out_specs, check_vma=False
    )
```
